256 devices in a mesh: owner: 64 (over z, x, core), helper: 4 (over y).
Axes of the slice: x: 4, y: 4, z: 8, core: 2. Of those that a mesh axis runs over, the one named last changes fastest.
Arguments:
- states: bfloat16 [128, 128, 768], P('owner'), may hold values from -6 to 6
- partners: int32 [128, 21], P('owner'), may hold values from -1 to 127, as said below
- self_proj: bfloat16 [3, 768, 768], P(None, None, 'helper'), may hold values from -0.28867513 to 0.28867513
- self_out: bfloat16 [768, 768], P('helper'), may hold values from -0.21875 to 0.21875
- cross_proj: bfloat16 [3, 768, 768], P(None, None, 'helper'), may hold values from -0.28867513 to 0.28867513
- cross_out: bfloat16 [768, 768], P('helper'), may hold values from -0.21875 to 0.21875
- gains: float32 [3, 768], replicated, may hold values from 0.5 to 1.5
Outputs:
- pair_states: bfloat16 [128, 21, 128, 768], P('owner', None, 'helper')
The draws below stay inside these ranges and needn't reach their ends.
Inputs may be any that keep to these rules, and one draw needn't show every extreme that they name: Row i lists the images paired with image i, left-aligned, then -1 in the remaining slots. Pairs are symmetric. Images 2 * o and 2 * o + 1 belong to owner o. With M = 64 owners, every pair joins owner o with owner o + k modulo M for k from 1 to 10 or k = M // 2, or with owner o - k modulo M for k from 1 to 10; each of these 21 owners is joined to o by exactly one pair, so the two images of one owner take part in exactly 21 pairs together, and some image has 21 partners.
All inputs are finite; a program needn't handle non-finite values.
Results may differ from the reference program's by a relative error of at most 0.0095.
Values may be sent and summed in bfloat16 or wider, within the bound.
A program may use at most 128 MiB of HBM per device.

```python
import jax
import jax.numpy as jnp
from jax import lax

D = 768
HEAD = 64
PATCHES = 128
NEAR = 11
SLOTS = 21
IMAGES = 128


def clipped_normal(key, shape, limit):
    return jnp.clip(jax.random.normal(key, shape, jnp.float32), -limit, limit)


def draw_states(key, part):
    key = jax.random.fold_in(key, 11)
    key_base = jax.random.fold_in(key, 0)
    values = clipped_normal(key_base, (IMAGES, PATCHES, D), 6.0)
    return values.astype(jnp.bfloat16)


def draw_self_proj(key, part):
    key = jax.random.fold_in(key, 23)
    scale = D ** (-0.5)
    values = clipped_normal(key, (3, D, D), 6.0) * scale
    return values.astype(jnp.bfloat16)


def draw_cross_proj(key, part):
    key = jax.random.fold_in(key, 37)
    scale = D ** (-0.5)
    values = clipped_normal(key, (3, D, D), 6.0) * scale
    return values.astype(jnp.bfloat16)


def draw_partners(key, part):
    key = jax.random.fold_in(key, 7)
    owner_count = IMAGES // 2
    half_way = owner_count // 2
    key_level, key_front, key_back = jax.random.split(key, 3)
    level = jax.random.randint(key_level, (owner_count,), 1, 10)
    owner_ids = jnp.arange(owner_count, dtype=jnp.int32)
    offsets = jnp.where(jnp.arange(NEAR, dtype=jnp.int32) == NEAR - 1, half_way, jnp.arange(1, NEAR + 1, dtype=jnp.int32)).astype(jnp.int32)
    is_half = (jnp.arange(NEAR, dtype=jnp.int32) == NEAR - 1)[None, :]
    starts = jnp.logical_or(jnp.logical_not(is_half), owner_ids[:, None] < half_way)
    target = (owner_ids[:, None] + offsets[None, :]) % owner_count
    front_bit = (jax.random.randint(key_front, (owner_count, NEAR), 0, 10) >= level[:, None]).astype(jnp.int32)
    back_bit = (jax.random.randint(key_back, (owner_count, NEAR), 0, 10) >= level[target]).astype(jnp.int32)
    front_bit = jnp.where(owner_ids[:, None] == 0, 0, front_bit)
    back_bit = jnp.where(target == 0, 0, back_bit)
    front_partner = 2 * target + back_bit
    anchor = (owner_ids[:, None] - offsets[None, :]) % owner_count
    offset_index = jnp.broadcast_to(jnp.arange(NEAR, dtype=jnp.int32)[None, :], anchor.shape)
    back_here = back_bit[anchor, offset_index]
    back_live = starts[anchor, offset_index]
    back_partner = 2 * anchor + front_bit[anchor, offset_index]
    listing = []
    for image_bit in range(2):
        forward_list = jnp.where(jnp.logical_and(front_bit == image_bit, starts), front_partner, -1)
        backward_list = jnp.where(jnp.logical_and(back_here == image_bit, back_live), back_partner, -1)
        listing.append(jnp.concatenate([forward_list, backward_list], axis=1))
    candidates = jnp.stack(listing, axis=1).astype(jnp.int32)
    sort_order = jnp.argsort((candidates < 0).astype(jnp.int32), axis=-1, stable=True)
    candidates = jnp.take_along_axis(candidates, sort_order, axis=-1)[:, :, :SLOTS]
    return candidates.reshape(IMAGES, SLOTS).astype(jnp.int32)


def levels(key, extent, pieces, smallest, top_value):
    level, own = 1.0, jax.random.fold_in(key, 6)
    for axis_at, parts in pieces:
        steps = jnp.exp(jax.random.uniform(jax.random.fold_in(own, axis_at), (parts,), jnp.float32, smallest / len(pieces), top_value / len(pieces)))
        level = level * jnp.repeat(steps, extent[axis_at] // parts).reshape([-1 if axis == axis_at else 1 for axis in range(len(extent))])
    return level


def bell_draw(stream_key, extent, deviation, reach, cuts=(), kind=jnp.bfloat16):
    entries = deviation * jax.random.normal(stream_key, extent, jnp.float32)
    if cuts:
        entries = entries * levels(stream_key, extent, cuts, -0.22, 0.18)
    return jnp.clip(entries, -reach, reach).astype(kind)


def setup_inputs(seed: int = 0) -> dict:
    seeds = jax.random.split(jax.random.key(seed), 8)
    return {
        "states": draw_states(jax.random.fold_in(seeds[7], 71), 0),
        "partners": draw_partners(jax.random.fold_in(seeds[7], 71), 0),
        "self_proj": draw_self_proj(jax.random.fold_in(seeds[7], 71), 0),
        "self_out": bell_draw(seeds[3], (D, D), D ** -0.5, 0.21875, ((0, 4),)),
        "cross_proj": draw_cross_proj(jax.random.fold_in(seeds[7], 71), 0),
        "cross_out": bell_draw(seeds[5], (D, D), D ** -0.5, 0.21875, ((0, 4),)),
        "gains": jnp.clip(1.0 + 0.1 * jax.random.normal(seeds[6], (3, D), jnp.float32), 0.5, 1.5),
    }


def rounded(values):
    return lax.optimization_barrier(values.astype(jnp.bfloat16)).astype(jnp.float32)

def norm_rows(values, gain_row):
    row_mean = lax.optimization_barrier(jnp.mean(values, -1, keepdims=True))
    centred = values - row_mean
    row_var = lax.optimization_barrier(jnp.mean(centred * centred, -1, keepdims=True))
    return centred * lax.rsqrt(row_var + 1e-05) * gain_row

def attend(queries, key_rows, value_rows):
    count_n, patch_n, column_n = queries.shape
    head_count = column_n // HEAD
    q_heads = queries.reshape(count_n, patch_n, head_count, HEAD)
    k_heads = key_rows.reshape(count_n, key_rows.shape[1], head_count, HEAD)
    v_heads = value_rows.reshape(count_n, value_rows.shape[1], head_count, HEAD)
    scores = jnp.einsum('nqhe,nkhe->nhqk', q_heads, k_heads) * HEAD ** (-0.5)
    weights = rounded(jax.nn.softmax(scores, axis=-1))
    context = jnp.einsum('nhqk,nkhe->nqhe', weights, v_heads)
    return rounded(context).reshape(count_n, patch_n, column_n)

def reference(states, partners, self_proj, self_out, cross_proj, cross_out, gains):
    as_float = states.astype(jnp.float32)
    normed = rounded(norm_rows(as_float, gains[0]))
    projected = rounded(jnp.einsum('ipd,cdf->cipf', normed, self_proj.astype(jnp.float32)))
    context = attend(projected[0], projected[1], projected[2])
    mixed = as_float + jnp.einsum('ipf,fd->ipd', context, self_out.astype(jnp.float32))
    queries = rounded(jnp.einsum('ipd,df->ipf', rounded(norm_rows(mixed, gains[1])), cross_proj[0].astype(jnp.float32)))
    key_norm = rounded(norm_rows(as_float, gains[2]))
    key_rows = rounded(jnp.einsum('ipd,df->ipf', key_norm, cross_proj[1].astype(jnp.float32)))
    value_rows = rounded(jnp.einsum('ipd,df->ipf', key_norm, cross_proj[2].astype(jnp.float32)))
    out_weight = cross_out.astype(jnp.float32)

    def one_image(inputs):
        image_query, image_mixed, image_partners = inputs
        is_live = image_partners >= 0
        picked = jnp.where(is_live, image_partners, 0).astype(jnp.int32)
        side_keys = key_rows[picked]
        side_values = value_rows[picked]
        side_query = jnp.broadcast_to(image_query[None], side_keys.shape)
        side_context = attend(side_query, side_keys, side_values)
        result = image_mixed[None] + jnp.einsum('spf,fd->spd', side_context, out_weight)
        result = jnp.where(is_live[:, None, None], result, jnp.zeros((), jnp.float32))
        return result.astype(jnp.bfloat16)
    return lax.map(one_image, (queries, mixed, partners))
```

```python
import functools

import jax
import jax.numpy as jnp
from jax import lax
from jax.experimental import pallas as pl
from jax.experimental.pallas import tpu as pltpu
from jax.sharding import PartitionSpec as P

MESH = pl.DeviceIdType.MESH
BF16 = jnp.bfloat16
F32 = jnp.float32

OWNERS = 64
HELPERS = 4
IMAGES = 2
PATCHES = 128
ROWS = PATCHES // HELPERS
D = 768
HEAD = 64
HEADS = 3
COLS = HEADS * HEAD
SLOTS = 21
NEAR = 10
PAIRS = 11
LANES = 2 * COLS
PAD = 64
VMEM_LIMIT = 56 * 1024 * 1024


def dot(a, b):
    return jnp.dot(a, b, preferred_element_type=F32)


def dot_nt(a, b):
    return lax.dot_general(a, b, (((1,), (1,)), ((), ())), preferred_element_type=F32)


def pair_tiles(first, second):
    zero = jnp.zeros((first.shape[0], HEAD), F32)
    f = [first[:, HEAD * h : HEAD * (h + 1)] for h in range(HEADS)]
    s = [zero] * HEADS if second is None else [second[:, HEAD * h : HEAD * (h + 1)] for h in range(HEADS)]
    tiles = []
    for parity in range(2):
        row = []
        for h in range(HEADS):
            ordered = (s[h], f[h]) if (h + parity) % 2 == 0 else (f[h], s[h])
            row.append(jnp.concatenate(ordered, axis=1).astype(BF16))
        tiles.append(row)
    return tiles


def head_context(q_tile, kv_tile):
    scores = dot_nt(q_tile, kv_tile)
    top = jnp.max(scores, axis=1, keepdims=True)
    weights = jnp.exp(scores - top)
    total = jnp.sum(weights, axis=1, keepdims=True)
    return dot(weights.astype(BF16), kv_tile) * (1.0 / total)


def join_contexts(even, odd):
    low = lax.broadcasted_iota(jnp.int32, (PATCHES, 2 * HEAD), 1) < HEAD
    if odd is None:
        odd = [even[0], even[1], even[0]]
    return (
        jnp.where(low, even[0], even[1]).astype(BF16),
        jnp.where(low, even[2], odd[0]).astype(BF16),
        jnp.where(low, odd[1], odd[2]).astype(BF16),
    )


def exchange_kernel(
    part,
    states_hbm,
    sproj_hbm,
    sout_hbm,
    cproj_hbm,
    cout_hbm,
    gains,
    ctx_out,
    w_out,
    mixed_out,
    states_v,
    sproj_v,
    cproj_v,
    sw,
    x0,
    x2,
    kvbuf,
    sendbuf,
    recvbuf,
    sctx,
    mixed_v,
    qbuf,
    ctxbuf,
    bits,
    in_sem,
    loc_sem,
    own_sem,
    kv_send,
    kv_recv,
    w_send,
    w_recv,
    f_send,
    f_recv,
    s_send,
    s_recv,
    c_send,
    c_recv,
):
    me = lax.axis_index("owner")
    my_h = lax.axis_index("helper")
    core = me % 2
    sibling = me + 1 - 2 * core

    def owner_at(offset):
        return (me + offset + OWNERS) % OWNERS

    def helper_at(step):
        return (my_h + step) % HELPERS

    barrier = pltpu.get_barrier_semaphore()

    @pl.loop(0, NEAR)
    def _(k):
        for sign in (1, -1):
            pl.semaphore_signal(
                barrier, inc=1, device_id=(owner_at(sign * (k + 1)), my_h), device_id_type=MESH
            )

    pl.semaphore_signal(barrier, inc=1, device_id=(owner_at(32), my_h), device_id_type=MESH)
    for step in range(1, HELPERS):
        pl.semaphore_signal(barrier, inc=1, device_id=(me, helper_at(step)), device_id_type=MESH)

    loads = [
        pltpu.make_async_copy(states_hbm, states_v, in_sem.at[0]),
        pltpu.make_async_copy(cproj_hbm, cproj_v, in_sem.at[1]),
        pltpu.make_async_copy(sproj_hbm, sproj_v, in_sem.at[2]),
        pltpu.make_async_copy(sout_hbm, sw.at[my_h, pl.ds(PAD, COLS)], in_sem.at[3]),
        pltpu.make_async_copy(cout_hbm, w_out.at[my_h], in_sem.at[4]),
    ]
    for load in loads:
        load.start()
    sw[:, 0:PAD] = jnp.zeros((HELPERS, PAD, D), BF16)
    sw[:, PAD + COLS :] = jnp.zeros((HELPERS, PAD, D), BF16)

    @pl.loop(0, SLOTS)
    def _(j):
        offset = jnp.where(j == SLOTS - 1, 32, (1 + j // 2) * (1 - 2 * (j % 2)))
        target = owner_at(offset)
        bit = jnp.int32(0)
        for s in range(SLOTS):
            p = part[1, s]
            hit = jnp.logical_and(p >= 2 * target, p <= 2 * target + 1)
            bit = jnp.where(hit, 1, bit)
        bits[j] = bit

    loads[0].wait()
    as_float = states_v[...].reshape(IMAGES * PATCHES, D).astype(F32)
    row_mean = jnp.mean(as_float, -1, keepdims=True)
    centred = as_float - row_mean
    row_var = jnp.mean(centred * centred, -1, keepdims=True)
    scaled = centred * lax.rsqrt(row_var + 1e-05)
    x2[...] = (scaled * gains[2:3, :]).astype(BF16)
    x0[...] = (scaled * gains[0:1, :]).astype(BF16)

    loads[1].wait()
    key_rows = dot(x2[...], cproj_v[1])
    value_rows = dot(x2[...], cproj_v[2])
    tiles = pair_tiles(key_rows, value_rows)
    for parity in range(2):
        for h in range(HEADS):
            for image in range(IMAGES):
                kvbuf[parity, image, :, 128 * h : 128 * (h + 1)] = tiles[parity][h][
                    PATCHES * image : PATCHES * (image + 1)
                ]

    pl.semaphore_wait(barrier, SLOTS + HELPERS - 1)

    def half(owner_core):
        return pl.ds(pl.multiple_of(owner_core * (COLS // 2), COLS // 2), COLS // 2)

    def self_rows(h, owner_core):
        return sw.at[h, pl.ds(pl.multiple_of(PAD + owner_core * (COLS // 2), 32), COLS // 2)]

    def weight_copy(which, step):
        source = sout_hbm if which == 0 else cout_hbm
        landing = self_rows(my_h, core) if which == 0 else w_out.at[my_h, half(core)]
        return pltpu.make_async_remote_copy(
            src_ref=source.at[half(core)],
            dst_ref=landing,
            send_sem=w_send.at[which, step - 1],
            recv_sem=w_recv.at[which, step - 1],
            device_id=(me, helper_at(step)),
            device_id_type=MESH,
        )

    def forward_copy(which, step):
        source = helper_at(HELPERS - step)
        block = self_rows(source, core) if which == 0 else w_out.at[source, half(core)]
        return pltpu.make_async_remote_copy(
            src_ref=block,
            dst_ref=block,
            send_sem=f_send.at[which, step - 1],
            recv_sem=f_recv.at[which, step - 1],
            device_id=(sibling, my_h),
            device_id_type=MESH,
        )

    def kv_copy(j, offset, landing):
        return pltpu.make_async_remote_copy(
            src_ref=sendbuf.at[j],
            dst_ref=recvbuf.at[landing],
            send_sem=kv_send.at[j],
            recv_sem=kv_recv.at[landing],
            device_id=(owner_at(offset), my_h),
            device_id_type=MESH,
        )

    for step in range(1, HELPERS):
        weight_copy(0, step).start()

    kv_copy_last = kv_copy(SLOTS - 1, 32, SLOTS - 1)
    sendbuf[SLOTS - 1] = kvbuf[0, bits[SLOTS - 1]]
    kv_copy_last.start()

    @pl.loop(0, NEAR)
    def _(k):
        sendbuf[2 * k] = kvbuf[1, bits[2 * k]]
        kv_copy(2 * k, k + 1, 2 * k + 1).start()
        sendbuf[2 * k + 1] = kvbuf[0, bits[2 * k + 1]]
        kv_copy(2 * k + 1, -(k + 1), 2 * k).start()

    for step in range(1, HELPERS):
        weight_copy(1, step).start()

    loads[2].wait()
    sq = dot(x0[...], sproj_v[0]) * HEAD ** (-0.5)
    sk = dot(x0[...], sproj_v[1])
    sv = dot(x0[...], sproj_v[2])
    q_tiles = pair_tiles(sq, None)
    kv_tiles = pair_tiles(sk, sv)
    contexts = []
    for image in range(IMAGES):
        rows = slice(PATCHES * image, PATCHES * (image + 1))
        contexts.append(
            [head_context(q_tiles[image][h][rows], kv_tiles[image][h][rows]) for h in range(HEADS)]
        )
    for t, tile in enumerate(join_contexts(*contexts)):
        sctx[my_h, :, 128 * t : 128 * (t + 1)] = tile

    def self_copy(step):
        return pltpu.make_async_remote_copy(
            src_ref=sctx.at[my_h],
            dst_ref=sctx.at[my_h],
            send_sem=s_send.at[step - 1],
            recv_sem=s_recv.at[step - 1],
            device_id=(me, helper_at(step)),
            device_id_type=MESH,
        )

    def self_arrival(step):
        source = helper_at(HELPERS - step)
        return pltpu.make_async_remote_copy(
            src_ref=sctx.at[source],
            dst_ref=sctx.at[source],
            send_sem=s_send.at[step - 1],
            recv_sem=s_recv.at[step - 1],
            device_id=(me, source),
            device_id_type=MESH,
        )

    def weight_arrival(which, step):
        source = helper_at(HELPERS - step)
        landed = self_rows(source, core) if which == 0 else w_out.at[source, half(core)]
        return pltpu.make_async_remote_copy(
            src_ref=landed,
            dst_ref=landed,
            send_sem=w_send.at[which, step - 1],
            recv_sem=w_recv.at[which, step - 1],
            device_id=(me, source),
            device_id_type=MESH,
        )

    def forward_arrival(which, step):
        source = helper_at(HELPERS - step)
        landed = self_rows(source, 1 - core) if which == 0 else w_out.at[source, half(1 - core)]
        return pltpu.make_async_remote_copy(
            src_ref=landed,
            dst_ref=landed,
            send_sem=f_send.at[which, step - 1],
            recv_sem=f_recv.at[which, step - 1],
            device_id=(sibling, my_h),
            device_id_type=MESH,
        )

    for step in range(1, HELPERS):
        self_copy(step).start()
    for step in range(1, HELPERS):
        weight_arrival(0, step).wait_recv()
        forward_copy(0, step).start()
    for step in range(1, HELPERS):
        forward_arrival(0, step).wait_recv()
    for step in range(1, HELPERS):
        self_arrival(step).wait_recv()
    loads[3].wait()

    for image in range(IMAGES):
        total = states_v[image].astype(F32)
        for h in range(HELPERS):
            if image == 0:
                total += dot(sctx[h, :, 0:256], sw[h, PAD:])
            else:
                total += dot(sctx[h, :, 128:384], sw[h, 0 : PAD + COLS])
        mixed_v[image] = total
        row_mean = jnp.mean(total, -1, keepdims=True)
        centred = total - row_mean
        row_var = jnp.mean(centred * centred, -1, keepdims=True)
        x0[PATCHES * image : PATCHES * (image + 1)] = (
            centred * lax.rsqrt(row_var + 1e-05) * gains[1:2, :]
        ).astype(BF16)

    def my_rows(helper):
        return pl.ds(pl.multiple_of(helper * ROWS, ROWS), ROWS)

    mixed_copy = pltpu.make_async_copy(mixed_v.at[:, my_rows(my_h)], mixed_out, loc_sem.at[0])
    mixed_copy.start()

    queries = dot(x0[...], cproj_v[0]) * HEAD ** (-0.5)
    q_tiles = pair_tiles(queries, None)
    for parity in range(2):
        for h in range(HEADS):
            for image in range(IMAGES):
                qbuf[parity, image, h] = q_tiles[parity][h][PATCHES * image : PATCHES * (image + 1)]

    def context_copy(pair, step):
        return pltpu.make_async_remote_copy(
            src_ref=ctxbuf.at[pair, my_rows(helper_at(step))],
            dst_ref=ctx_out.at[my_h, pair],
            send_sem=c_send.at[pair, step - 1],
            recv_sem=c_recv.at[pair, step - 1],
            device_id=(me, helper_at(step)),
            device_id_type=MESH,
        )

    def context_arrival(pair, step):
        source = helper_at(HELPERS - step)
        return pltpu.make_async_remote_copy(
            src_ref=ctxbuf.at[pair, my_rows(my_h)],
            dst_ref=ctx_out.at[source, pair],
            send_sem=c_send.at[pair, step - 1],
            recv_sem=c_recv.at[pair, step - 1],
            device_id=(me, source),
            device_id_type=MESH,
        )

    def own_copy(pair):
        return pltpu.make_async_copy(
            ctxbuf.at[pair, my_rows(my_h)], ctx_out.at[my_h, pair], own_sem.at[pair]
        )

    def kv_arrival(j, offset):
        return pltpu.make_async_remote_copy(
            src_ref=sendbuf.at[j],
            dst_ref=recvbuf.at[j],
            send_sem=kv_send.at[j],
            recv_sem=kv_recv.at[j],
            device_id=(owner_at(offset), my_h),
            device_id_type=MESH,
        )

    def slot_contexts(j, parity):
        image = bits[j]
        return [
            head_context(qbuf[parity, image, h], recvbuf[j, :, 128 * h : 128 * (h + 1)])
            for h in range(HEADS)
        ]

    def finish_pair(pair, even, odd):
        for t, tile in enumerate(join_contexts(even, odd)):
            ctxbuf[pair, :, 128 * t : 128 * (t + 1)] = tile
        for step in range(1, HELPERS):
            context_copy(pair, step).start()
        own_copy(pair).start()

    @pl.loop(0, NEAR)
    def _(pair):
        kv_arrival(2 * pair, pair + 1).wait_recv()
        even = slot_contexts(2 * pair, 0)
        kv_arrival(2 * pair + 1, -(pair + 1)).wait_recv()
        odd = slot_contexts(2 * pair + 1, 1)
        finish_pair(pair, even, odd)

    kv_arrival(SLOTS - 1, 32).wait_recv()
    finish_pair(PAIRS - 1, slot_contexts(SLOTS - 1, 0), None)

    for step in range(1, HELPERS):
        weight_arrival(1, step).wait_recv()
        forward_copy(1, step).start()
    for step in range(1, HELPERS):
        forward_arrival(1, step).wait_recv()
    loads[4].wait()
    mixed_copy.wait()
    for step in range(1, HELPERS):
        self_copy(step).wait_send()
        for which in range(2):
            weight_copy(which, step).wait_send()
            forward_copy(which, step).wait_send()

    @pl.loop(0, NEAR)
    def _(k):
        kv_copy(2 * k, k + 1, 2 * k + 1).wait_send()
        kv_copy(2 * k + 1, -(k + 1), 2 * k).wait_send()

    kv_copy_last.wait_send()

    @pl.loop(0, PAIRS)
    def _(pair):
        for step in range(1, HELPERS):
            context_copy(pair, step).wait_send()
            context_arrival(pair, step).wait_recv()
        own_copy(pair).wait()


def place_kernel(
    part, ctx_hbm, w_hbm, mixed, out, ctx, w, terms, result, blank, ctx_sem, w_sem, out_sem
):
    me = lax.axis_index("owner")
    load_w = pltpu.make_async_copy(w_hbm, w.at[:, pl.ds(PAD, COLS)], w_sem)
    load_ctx = pltpu.make_async_copy(ctx_hbm, ctx, ctx_sem)
    load_w.start()
    load_ctx.start()
    w[:, 0:PAD] = jnp.zeros((HELPERS, PAD, D), BF16)
    w[:, PAD + COLS :] = jnp.zeros((HELPERS, PAD, D), BF16)
    blank[...] = jnp.zeros((ROWS, D), BF16)
    load_w.wait()
    load_ctx.wait()
    for parity in range(2):
        total = None
        for h in range(HELPERS):
            if parity == 0:
                term = dot(ctx[h, :, :, 0:256].reshape(PAIRS * ROWS, 256), w[h, PAD:])
            else:
                term = dot(ctx[h, :, :, 128:384].reshape(PAIRS * ROWS, 256), w[h, 0 : PAD + COLS])
            total = term if total is None else total + term
        terms[parity] = total.reshape(PAIRS, ROWS, D)

    def out_copy(source, image, slot):
        return pltpu.make_async_copy(source, out.at[image, slot], out_sem.at[image, slot])

    for image in range(IMAGES):

        @pl.loop(0, SLOTS)
        def _(slot):
            p = part[image, slot]
            offset = (lax.div(jnp.maximum(p, 0), 2) - me + OWNERS) % OWNERS
            far = offset == 32
            back = offset > 32
            pair = jnp.where(far, PAIRS - 1, jnp.where(back, OWNERS - offset, offset) - 1)
            pair = jnp.clip(pair, 0, PAIRS - 1)
            parity = jnp.where(back, 1, 0)

            @pl.when(p >= 0)
            def _():
                result[image, slot] = (terms[parity, pair] + mixed[image]).astype(BF16)
                out_copy(result.at[image, slot], image, slot).start()

            @pl.when(p < 0)
            def _():
                out_copy(blank, image, slot).start()

    for image in range(IMAGES):

        @pl.loop(0, SLOTS)
        def _(slot):
            out_copy(blank, image, slot).wait()


def local(states, partners, self_proj, self_out, cross_proj, cross_out, gains):
    any_spec = pl.BlockSpec(memory_space=pl.ANY)
    smem = pl.BlockSpec(memory_space=pltpu.SMEM)
    vmem = pl.BlockSpec(memory_space=pltpu.VMEM)
    dma = pltpu.SemaphoreType.DMA
    ctx, weight, mixed = pl.pallas_call(
        exchange_kernel,
        out_shape=(
            jax.ShapeDtypeStruct((HELPERS, PAIRS, ROWS, LANES), BF16),
            jax.ShapeDtypeStruct((HELPERS, COLS, D), BF16),
            jax.ShapeDtypeStruct((IMAGES, ROWS, D), F32),
        ),
        in_specs=[smem, any_spec, any_spec, any_spec, any_spec, any_spec, vmem],
        out_specs=(any_spec, any_spec, any_spec),
        scratch_shapes=[
            pltpu.VMEM((IMAGES, PATCHES, D), BF16),
            pltpu.VMEM((3, D, COLS), BF16),
            pltpu.VMEM((3, D, COLS), BF16),
            pltpu.VMEM((HELPERS, COLS + 2 * PAD, D), BF16),
            pltpu.VMEM((IMAGES * PATCHES, D), BF16),
            pltpu.VMEM((IMAGES * PATCHES, D), BF16),
            pltpu.VMEM((2, IMAGES, PATCHES, LANES), BF16),
            pltpu.VMEM((SLOTS, PATCHES, LANES), BF16),
            pltpu.VMEM((SLOTS, PATCHES, LANES), BF16),
            pltpu.VMEM((HELPERS, PATCHES, LANES), BF16),
            pltpu.VMEM((IMAGES, PATCHES, D), F32),
            pltpu.VMEM((2, IMAGES, HEADS, PATCHES, 2 * HEAD), BF16),
            pltpu.VMEM((PAIRS, PATCHES, LANES), BF16),
            pltpu.SMEM((SLOTS,), jnp.int32),
            dma((5,)),
            dma((1,)),
            dma((PAIRS,)),
            dma((SLOTS,)),
            dma((SLOTS,)),
            dma((2, 3)),
            dma((2, 3)),
            dma((2, 3)),
            dma((2, 3)),
            dma((3,)),
            dma((3,)),
            dma((PAIRS, 3)),
            dma((PAIRS, 3)),
        ],
        compiler_params=pltpu.CompilerParams(
            collective_id=0, has_side_effects=True, vmem_limit_bytes=VMEM_LIMIT
        ),
        name="exchange",
    )(partners, states, self_proj, self_out, cross_proj, cross_out, gains)
    return pl.pallas_call(
        place_kernel,
        out_shape=jax.ShapeDtypeStruct((IMAGES, SLOTS, ROWS, D), BF16),
        in_specs=[smem, any_spec, any_spec, vmem],
        out_specs=any_spec,
        scratch_shapes=[
            pltpu.VMEM((HELPERS, PAIRS, ROWS, LANES), BF16),
            pltpu.VMEM((HELPERS, COLS + 2 * PAD, D), BF16),
            pltpu.VMEM((2, PAIRS, ROWS, D), F32),
            pltpu.VMEM((IMAGES, SLOTS, ROWS, D), BF16),
            pltpu.VMEM((ROWS, D), BF16),
            dma,
            dma,
            dma((IMAGES, SLOTS)),
        ],
        compiler_params=pltpu.CompilerParams(vmem_limit_bytes=VMEM_LIMIT),
        name="place",
    )(partners, ctx, weight, mixed)


def solution(mesh):
    return jax.shard_map(
        local,
        mesh=mesh,
        in_specs=(
            P("owner", None, None),
            P("owner", None),
            P(None, None, "helper"),
            P("helper", None),
            P(None, None, "helper"),
            P("helper", None),
            P(),
        ),
        out_specs=P("owner", None, "helper", None),
        check_vma=False,
    )
```

```python
import functools

import jax
import jax.numpy as jnp
from jax import lax
from jax.experimental import pallas as pl
from jax.experimental.pallas import tpu as pltpu
from jax.sharding import PartitionSpec as P

MESH = pl.DeviceIdType.MESH
BF16 = jnp.bfloat16
F32 = jnp.float32

OWNERS = 64
HELPERS = 4
IMAGES = 2
PATCHES = 128
ROWS = PATCHES // HELPERS
D = 768
HEAD = 64
HEADS = 3
COLS = HEADS * HEAD
SLOTS = 21
NEAR = 10
PAIRS = 11
LANES = 2 * COLS
PAD = 64
VMEM_LIMIT = 56 * 1024 * 1024


def dot(a, b):
    return jnp.dot(a, b, preferred_element_type=F32)


def dot_nt(a, b):
    return lax.dot_general(a, b, (((1,), (1,)), ((), ())), preferred_element_type=F32)


def pair_tiles(first, second):
    zero = jnp.zeros((first.shape[0], HEAD), F32)
    f = [first[:, HEAD * h : HEAD * (h + 1)] for h in range(HEADS)]
    s = [zero] * HEADS if second is None else [second[:, HEAD * h : HEAD * (h + 1)] for h in range(HEADS)]
    tiles = []
    for parity in range(2):
        row = []
        for h in range(HEADS):
            ordered = (s[h], f[h]) if (h + parity) % 2 == 0 else (f[h], s[h])
            row.append(jnp.concatenate(ordered, axis=1).astype(BF16))
        tiles.append(row)
    return tiles


def head_contexts(tiles):
    scores = [dot_nt(q, kv) for q, kv in tiles]
    weights = [jnp.exp(s - jnp.max(s, axis=1, keepdims=True)) for s in scores]
    totals = [jnp.sum(w, axis=1, keepdims=True) for w in weights]
    return [
        dot(w.astype(BF16), kv) * (1.0 / t) for w, t, (_, kv) in zip(weights, totals, tiles)
    ]


def join_contexts(even, odd):
    low = lax.broadcasted_iota(jnp.int32, (PATCHES, 2 * HEAD), 1) < HEAD
    if odd is None:
        odd = [even[0], even[1], even[0]]
    return (
        jnp.where(low, even[0], even[1]).astype(BF16),
        jnp.where(low, even[2], odd[0]).astype(BF16),
        jnp.where(low, odd[1], odd[2]).astype(BF16),
    )


def exchange_kernel(
    part,
    states_hbm,
    sproj_hbm,
    sout_hbm,
    cproj_hbm,
    cout_hbm,
    gains,
    ctx_out,
    w_out,
    mixed_out,
    states_v,
    sproj_v,
    cproj_v,
    sw,
    x0,
    x2,
    kvbuf,
    sendbuf,
    recvbuf,
    sctx,
    mixed_v,
    qbuf,
    ctxbuf,
    bits,
    in_sem,
    loc_sem,
    own_sem,
    kv_send,
    kv_recv,
    w_send,
    w_recv,
    f_send,
    f_recv,
    s_send,
    s_recv,
    c_send,
    c_recv,
):
    me = lax.axis_index("owner")
    my_h = lax.axis_index("helper")
    core = me % 2
    sibling = me + 1 - 2 * core

    def owner_at(offset):
        return (me + offset + OWNERS) % OWNERS

    def helper_at(step):
        return (my_h + step) % HELPERS

    barrier = pltpu.get_barrier_semaphore()

    @pl.loop(0, NEAR)
    def _(k):
        for sign in (1, -1):
            pl.semaphore_signal(
                barrier, inc=1, device_id=(owner_at(sign * (k + 1)), my_h), device_id_type=MESH
            )

    pl.semaphore_signal(barrier, inc=1, device_id=(owner_at(32), my_h), device_id_type=MESH)
    for step in range(1, HELPERS):
        pl.semaphore_signal(barrier, inc=1, device_id=(me, helper_at(step)), device_id_type=MESH)

    loads = [
        pltpu.make_async_copy(states_hbm, states_v, in_sem.at[0]),
        pltpu.make_async_copy(cproj_hbm, cproj_v, in_sem.at[1]),
        pltpu.make_async_copy(sproj_hbm, sproj_v, in_sem.at[2]),
        pltpu.make_async_copy(sout_hbm, sw.at[my_h, pl.ds(PAD, COLS)], in_sem.at[3]),
        pltpu.make_async_copy(cout_hbm, w_out.at[my_h], in_sem.at[4]),
    ]
    for load in loads:
        load.start()
    sw[:, 0:PAD] = jnp.zeros((HELPERS, PAD, D), BF16)
    sw[:, PAD + COLS :] = jnp.zeros((HELPERS, PAD, D), BF16)

    @pl.loop(0, SLOTS)
    def _(j):
        offset = jnp.where(j == SLOTS - 1, 32, (1 + j // 2) * (1 - 2 * (j % 2)))
        target = owner_at(offset)
        bit = jnp.int32(0)
        for s in range(SLOTS):
            p = part[1, s]
            hit = jnp.logical_and(p >= 2 * target, p <= 2 * target + 1)
            bit = jnp.where(hit, 1, bit)
        bits[j] = bit

    loads[0].wait()
    as_float = states_v[...].reshape(IMAGES * PATCHES, D).astype(F32)
    row_mean = jnp.mean(as_float, -1, keepdims=True)
    centred = as_float - row_mean
    row_var = jnp.mean(centred * centred, -1, keepdims=True)
    scaled = centred * lax.rsqrt(row_var + 1e-05)
    x2[...] = (scaled * gains[2:3, :]).astype(BF16)
    x0[...] = (scaled * gains[0:1, :]).astype(BF16)

    loads[1].wait()
    key_rows = dot_nt(x2[...], cproj_v[1])
    value_rows = dot_nt(x2[...], cproj_v[2])
    tiles = pair_tiles(key_rows, value_rows)
    for parity in range(2):
        for h in range(HEADS):
            for image in range(IMAGES):
                kvbuf[parity, image, :, 128 * h : 128 * (h + 1)] = tiles[parity][h][
                    PATCHES * image : PATCHES * (image + 1)
                ]

    pl.semaphore_wait(barrier, SLOTS + HELPERS - 1)

    def half(owner_core):
        return pl.ds(pl.multiple_of(owner_core * (COLS // 2), COLS // 2), COLS // 2)

    def self_rows(h, owner_core):
        return sw.at[h, pl.ds(pl.multiple_of(PAD + owner_core * (COLS // 2), 32), COLS // 2)]

    def weight_copy(which, step):
        source = sout_hbm if which == 0 else cout_hbm
        landing = self_rows(my_h, core) if which == 0 else w_out.at[my_h, half(core)]
        return pltpu.make_async_remote_copy(
            src_ref=source.at[half(core)],
            dst_ref=landing,
            send_sem=w_send.at[which, step - 1],
            recv_sem=w_recv.at[which, step - 1],
            device_id=(me, helper_at(step)),
            device_id_type=MESH,
        )

    def forward_copy(which, step):
        source = helper_at(HELPERS - step)
        block = self_rows(source, core) if which == 0 else w_out.at[source, half(core)]
        return pltpu.make_async_remote_copy(
            src_ref=block,
            dst_ref=block,
            send_sem=f_send.at[which, step - 1],
            recv_sem=f_recv.at[which, step - 1],
            device_id=(sibling, my_h),
            device_id_type=MESH,
        )

    def kv_copy(j, offset, landing):
        return pltpu.make_async_remote_copy(
            src_ref=sendbuf.at[j],
            dst_ref=recvbuf.at[landing],
            send_sem=kv_send.at[j],
            recv_sem=kv_recv.at[landing],
            device_id=(owner_at(offset), my_h),
            device_id_type=MESH,
        )

    for step in range(1, HELPERS):
        weight_copy(0, step).start()

    kv_copy_last = kv_copy(SLOTS - 1, 32, SLOTS - 1)
    sendbuf[SLOTS - 1] = kvbuf[0, bits[SLOTS - 1]]
    kv_copy_last.start()

    @pl.loop(0, NEAR)
    def _(k):
        sendbuf[2 * k] = kvbuf[1, bits[2 * k]]
        kv_copy(2 * k, k + 1, 2 * k + 1).start()
        sendbuf[2 * k + 1] = kvbuf[0, bits[2 * k + 1]]
        kv_copy(2 * k + 1, -(k + 1), 2 * k).start()

    for step in range(1, HELPERS):
        weight_copy(1, step).start()

    loads[2].wait()
    sq = dot_nt(x0[...], sproj_v[0]) * HEAD ** (-0.5)
    sk = dot_nt(x0[...], sproj_v[1])
    sv = dot_nt(x0[...], sproj_v[2])
    q_tiles = pair_tiles(sq, None)
    kv_tiles = pair_tiles(sk, sv)
    pieces = [slice(PATCHES * image, PATCHES * (image + 1)) for image in range(IMAGES)]
    contexts = head_contexts(
        [
            (q_tiles[image][h][pieces[image]], kv_tiles[image][h][pieces[image]])
            for image in range(IMAGES)
            for h in range(HEADS)
        ]
    )
    for t, tile in enumerate(join_contexts(contexts[:HEADS], contexts[HEADS:])):
        sctx[my_h, :, 128 * t : 128 * (t + 1)] = tile

    def self_copy(step):
        return pltpu.make_async_remote_copy(
            src_ref=sctx.at[my_h],
            dst_ref=sctx.at[my_h],
            send_sem=s_send.at[step - 1],
            recv_sem=s_recv.at[step - 1],
            device_id=(me, helper_at(step)),
            device_id_type=MESH,
        )

    def self_arrival(step):
        source = helper_at(HELPERS - step)
        return pltpu.make_async_remote_copy(
            src_ref=sctx.at[source],
            dst_ref=sctx.at[source],
            send_sem=s_send.at[step - 1],
            recv_sem=s_recv.at[step - 1],
            device_id=(me, source),
            device_id_type=MESH,
        )

    def weight_arrival(which, step):
        source = helper_at(HELPERS - step)
        landed = self_rows(source, core) if which == 0 else w_out.at[source, half(core)]
        return pltpu.make_async_remote_copy(
            src_ref=landed,
            dst_ref=landed,
            send_sem=w_send.at[which, step - 1],
            recv_sem=w_recv.at[which, step - 1],
            device_id=(me, source),
            device_id_type=MESH,
        )

    def forward_arrival(which, step):
        source = helper_at(HELPERS - step)
        landed = self_rows(source, 1 - core) if which == 0 else w_out.at[source, half(1 - core)]
        return pltpu.make_async_remote_copy(
            src_ref=landed,
            dst_ref=landed,
            send_sem=f_send.at[which, step - 1],
            recv_sem=f_recv.at[which, step - 1],
            device_id=(sibling, my_h),
            device_id_type=MESH,
        )

    for step in range(1, HELPERS):
        self_copy(step).start()
    for step in range(1, HELPERS):
        weight_arrival(0, step).wait_recv()
        forward_copy(0, step).start()
    for step in range(1, HELPERS):
        forward_arrival(0, step).wait_recv()
    for step in range(1, HELPERS):
        self_arrival(step).wait_recv()
    loads[3].wait()

    for image in range(IMAGES):
        total = states_v[image].astype(F32)
        for h in range(HELPERS):
            if image == 0:
                total += dot(sctx[h, :, 0:256], sw[h, PAD:])
            else:
                total += dot(sctx[h, :, 128:384], sw[h, 0 : PAD + COLS])
        mixed_v[image] = total
        row_mean = jnp.mean(total, -1, keepdims=True)
        centred = total - row_mean
        row_var = jnp.mean(centred * centred, -1, keepdims=True)
        x0[PATCHES * image : PATCHES * (image + 1)] = (
            centred * lax.rsqrt(row_var + 1e-05) * gains[1:2, :]
        ).astype(BF16)

    def my_rows(helper):
        return pl.ds(pl.multiple_of(helper * ROWS, ROWS), ROWS)

    mixed_copy = pltpu.make_async_copy(mixed_v.at[:, my_rows(my_h)], mixed_out, loc_sem.at[0])
    mixed_copy.start()

    queries = dot_nt(x0[...], cproj_v[0]) * HEAD ** (-0.5)
    q_tiles = pair_tiles(queries, None)
    for parity in range(2):
        for h in range(HEADS):
            for image in range(IMAGES):
                qbuf[parity, image, h] = q_tiles[parity][h][PATCHES * image : PATCHES * (image + 1)]

    def context_copy(pair, step):
        return pltpu.make_async_remote_copy(
            src_ref=ctxbuf.at[pair, my_rows(helper_at(step))],
            dst_ref=ctx_out.at[my_h, pair],
            send_sem=c_send.at[pair, step - 1],
            recv_sem=c_recv.at[pair, step - 1],
            device_id=(me, helper_at(step)),
            device_id_type=MESH,
        )

    def context_arrival(pair, step):
        source = helper_at(HELPERS - step)
        return pltpu.make_async_remote_copy(
            src_ref=ctxbuf.at[pair, my_rows(my_h)],
            dst_ref=ctx_out.at[source, pair],
            send_sem=c_send.at[pair, step - 1],
            recv_sem=c_recv.at[pair, step - 1],
            device_id=(me, source),
            device_id_type=MESH,
        )

    def own_copy(pair):
        return pltpu.make_async_copy(
            ctxbuf.at[pair, my_rows(my_h)], ctx_out.at[my_h, pair], own_sem.at[pair]
        )

    def kv_arrival(j, offset):
        return pltpu.make_async_remote_copy(
            src_ref=sendbuf.at[j],
            dst_ref=recvbuf.at[j],
            send_sem=kv_send.at[j],
            recv_sem=kv_recv.at[j],
            device_id=(owner_at(offset), my_h),
            device_id_type=MESH,
        )

    def slot_tiles(j, parity):
        image = bits[j]
        return [
            (qbuf[parity, image, h], recvbuf[j, :, 128 * h : 128 * (h + 1)]) for h in range(HEADS)
        ]

    def finish_pair(pair, even, odd):
        for t, tile in enumerate(join_contexts(even, odd)):
            ctxbuf[pair, :, 128 * t : 128 * (t + 1)] = tile
        for step in range(1, HELPERS):
            context_copy(pair, step).start()
        own_copy(pair).start()

    @pl.loop(0, NEAR)
    def _(pair):
        kv_arrival(2 * pair, pair + 1).wait_recv()
        kv_arrival(2 * pair + 1, -(pair + 1)).wait_recv()
        contexts = head_contexts(slot_tiles(2 * pair, 0) + slot_tiles(2 * pair + 1, 1))
        finish_pair(pair, contexts[:HEADS], contexts[HEADS:])

    kv_arrival(SLOTS - 1, 32).wait_recv()
    finish_pair(PAIRS - 1, head_contexts(slot_tiles(SLOTS - 1, 0)), None)

    for step in range(1, HELPERS):
        weight_arrival(1, step).wait_recv()
        forward_copy(1, step).start()
    for step in range(1, HELPERS):
        forward_arrival(1, step).wait_recv()
    loads[4].wait()
    mixed_copy.wait()
    for step in range(1, HELPERS):
        self_copy(step).wait_send()
        for which in range(2):
            weight_copy(which, step).wait_send()
            forward_copy(which, step).wait_send()

    @pl.loop(0, NEAR)
    def _(k):
        kv_copy(2 * k, k + 1, 2 * k + 1).wait_send()
        kv_copy(2 * k + 1, -(k + 1), 2 * k).wait_send()

    kv_copy_last.wait_send()

    @pl.loop(0, PAIRS)
    def _(pair):
        for step in range(1, HELPERS):
            context_copy(pair, step).wait_send()
            context_arrival(pair, step).wait_recv()
        own_copy(pair).wait()


def place_kernel(
    part, ctx_hbm, w_hbm, mixed, out, ctx, w, result, blank, places, ctx_sem, w_sem, out_sem, blank_sem
):
    me = lax.axis_index("owner")
    load_w = pltpu.make_async_copy(w_hbm, w.at[:, pl.ds(PAD, COLS)], w_sem)
    load_ctx = pltpu.make_async_copy(ctx_hbm, ctx, ctx_sem)
    load_w.start()
    load_ctx.start()
    w[:, 0:PAD] = jnp.zeros((HELPERS, PAD, D), BF16)
    w[:, PAD + COLS :] = jnp.zeros((HELPERS, PAD, D), BF16)
    blank[...] = jnp.zeros((ROWS, D), BF16)

    def blank_copy(image, slot):
        return pltpu.make_async_copy(blank, out.at[image, slot], blank_sem.at[image, slot])

    for image in range(IMAGES):

        @pl.loop(0, SLOTS)
        def _(slot):
            p = part[image, slot]
            offset = (lax.div(jnp.maximum(p, 0), 2) - me + OWNERS) % OWNERS
            back = offset > 32
            near = jnp.where(back, 2 * (OWNERS - offset) - 1, 2 * offset - 2)
            index = jnp.clip(jnp.where(offset == 32, SLOTS - 1, near), 0, SLOTS - 1)

            @pl.when(p >= 0)
            def _():
                places[index] = image * SLOTS + slot

            @pl.when(p < 0)
            def _():
                blank_copy(image, slot).start()

    load_w.wait()
    load_ctx.wait()

    def out_copy(index):
        place = places[index]
        return pltpu.make_async_copy(
            result.at[index],
            out.at[lax.div(place, SLOTS), lax.rem(place, SLOTS)],
            out_sem.at[index],
        )

    for first, count in ((0, 6), (6, 5)):
        for parity in range(2):
            start, weight_rows = (0, slice(PAD, None)) if parity == 0 else (128, slice(0, 256))
            lhs = jnp.concatenate(
                [
                    ctx[h, first : first + count, :, start : start + 256].reshape(count * ROWS, 256)
                    for h in range(HELPERS)
                ],
                axis=1,
            )
            rhs = jnp.concatenate([w[h, weight_rows] for h in range(HELPERS)], axis=0)
            terms = dot(lhs, rhs)
            for n in range(count):
                index = 2 * (first + n) + parity
                if index < SLOTS:
                    image = lax.div(places[index], SLOTS)
                    result[index] = (terms[ROWS * n : ROWS * (n + 1)] + mixed[image]).astype(BF16)
                    out_copy(index).start()

    @pl.loop(0, SLOTS)
    def _(index):
        out_copy(index).wait()

    for image in range(IMAGES):

        @pl.loop(0, SLOTS)
        def _(slot):
            @pl.when(part[image, slot] < 0)
            def _():
                blank_copy(image, slot).wait()


def local(states, partners, self_proj, self_out, cross_proj, cross_out, gains):
    any_spec = pl.BlockSpec(memory_space=pl.ANY)
    smem = pl.BlockSpec(memory_space=pltpu.SMEM)
    vmem = pl.BlockSpec(memory_space=pltpu.VMEM)
    dma = pltpu.SemaphoreType.DMA
    ctx, weight, mixed = pl.pallas_call(
        exchange_kernel,
        out_shape=(
            jax.ShapeDtypeStruct((HELPERS, PAIRS, ROWS, LANES), BF16),
            jax.ShapeDtypeStruct((HELPERS, COLS, D), BF16),
            jax.ShapeDtypeStruct((IMAGES, ROWS, D), F32),
        ),
        in_specs=[smem, any_spec, any_spec, any_spec, any_spec, any_spec, vmem],
        out_specs=(any_spec, any_spec, any_spec),
        scratch_shapes=[
            pltpu.VMEM((IMAGES, PATCHES, D), BF16),
            pltpu.VMEM((3, COLS, D), BF16),
            pltpu.VMEM((3, COLS, D), BF16),
            pltpu.VMEM((HELPERS, COLS + 2 * PAD, D), BF16),
            pltpu.VMEM((IMAGES * PATCHES, D), BF16),
            pltpu.VMEM((IMAGES * PATCHES, D), BF16),
            pltpu.VMEM((2, IMAGES, PATCHES, LANES), BF16),
            pltpu.VMEM((SLOTS, PATCHES, LANES), BF16),
            pltpu.VMEM((SLOTS, PATCHES, LANES), BF16),
            pltpu.VMEM((HELPERS, PATCHES, LANES), BF16),
            pltpu.VMEM((IMAGES, PATCHES, D), F32),
            pltpu.VMEM((2, IMAGES, HEADS, PATCHES, 2 * HEAD), BF16),
            pltpu.VMEM((PAIRS, PATCHES, LANES), BF16),
            pltpu.SMEM((SLOTS,), jnp.int32),
            dma((5,)),
            dma((1,)),
            dma((PAIRS,)),
            dma((SLOTS,)),
            dma((SLOTS,)),
            dma((2, 3)),
            dma((2, 3)),
            dma((2, 3)),
            dma((2, 3)),
            dma((3,)),
            dma((3,)),
            dma((PAIRS, 3)),
            dma((PAIRS, 3)),
        ],
        compiler_params=pltpu.CompilerParams(
            collective_id=0, has_side_effects=True, vmem_limit_bytes=VMEM_LIMIT
        ),
        name="exchange",
    )(
        partners,
        states,
        jnp.swapaxes(self_proj, 1, 2),
        self_out,
        jnp.swapaxes(cross_proj, 1, 2),
        cross_out,
        gains,
    )
    return pl.pallas_call(
        place_kernel,
        out_shape=jax.ShapeDtypeStruct((IMAGES, SLOTS, ROWS, D), BF16),
        in_specs=[smem, any_spec, any_spec, vmem],
        out_specs=any_spec,
        scratch_shapes=[
            pltpu.VMEM((HELPERS, PAIRS, ROWS, LANES), BF16),
            pltpu.VMEM((HELPERS, COLS + 2 * PAD, D), BF16),
            pltpu.VMEM((SLOTS, ROWS, D), BF16),
            pltpu.VMEM((ROWS, D), BF16),
            pltpu.SMEM((SLOTS,), jnp.int32),
            dma,
            dma,
            dma((SLOTS,)),
            dma((IMAGES, SLOTS)),
        ],
        compiler_params=pltpu.CompilerParams(vmem_limit_bytes=VMEM_LIMIT),
        name="place",
    )(partners, ctx, weight, mixed)


def solution(mesh):
    return jax.shard_map(
        local,
        mesh=mesh,
        in_specs=(
            P("owner", None, None),
            P("owner", None),
            P(None, None, "helper"),
            P("helper", None),
            P(None, None, "helper"),
            P("helper", None),
            P(),
        ),
        out_specs=P("owner", None, "helper", None),
        check_vma=False,
    )
```

```python
import functools

import jax
import jax.numpy as jnp
from jax import lax
from jax.experimental import pallas as pl
from jax.experimental.pallas import tpu as pltpu
from jax.sharding import PartitionSpec as P

MESH = pl.DeviceIdType.MESH
BF16 = jnp.bfloat16
F32 = jnp.float32

OWNERS = 64
HELPERS = 4
IMAGES = 2
PATCHES = 128
ROWS = PATCHES // HELPERS
D = 768
HEAD = 64
HEADS = 3
COLS = HEADS * HEAD
SLOTS = 21
X, Z = 4, 8
PAIRS = 11
ACROSS = 80
WPIECE = COLS // X
LANES = 2 * COLS
PAD = 64
COPIES = 56
VMEM_LIMIT = 56 * 1024 * 1024


def dot(a, b):
    return jnp.dot(a, b, preferred_element_type=F32)


def dot_nt(a, b):
    return lax.dot_general(a, b, (((1,), (1,)), ((), ())), preferred_element_type=F32)


def pair_tiles(first, second):
    zero = jnp.zeros((first.shape[0], HEAD), F32)
    f = [first[:, HEAD * h : HEAD * (h + 1)] for h in range(HEADS)]
    s = [zero] * HEADS if second is None else [second[:, HEAD * h : HEAD * (h + 1)] for h in range(HEADS)]
    tiles = []
    for parity in range(2):
        row = []
        for h in range(HEADS):
            ordered = (s[h], f[h]) if (h + parity) % 2 == 0 else (f[h], s[h])
            row.append(jnp.concatenate(ordered, axis=1).astype(BF16))
        tiles.append(row)
    return tiles


def head_contexts(tiles):
    scores = [dot_nt(q, kv) for q, kv in tiles]
    weights = [jnp.exp(s - jnp.max(s, axis=1, keepdims=True)) for s in scores]
    totals = [jnp.sum(w, axis=1, keepdims=True) for w in weights]
    return [
        dot(w.astype(BF16), kv) * (1.0 / t) for w, t, (_, kv) in zip(weights, totals, tiles)
    ]


def join_contexts(even, odd):
    low = lax.broadcasted_iota(jnp.int32, (PATCHES, 2 * HEAD), 1) < HEAD
    if odd is None:
        odd = [even[0], even[1], even[0]]
    return (
        jnp.where(low, even[0], even[1]).astype(BF16),
        jnp.where(low, even[2], odd[0]).astype(BF16),
        jnp.where(low, odd[1], odd[2]).astype(BF16),
    )


def slot_owner(pair, parity, core):
    group = pair // 2
    size = jnp.where(group == 0, 4, jnp.where(group == 1, 1, jnp.where(group == 2, 3, 2)))
    both = 10 * core - 5
    single = jnp.where(parity == 0, 5 * (1 - core), -5 * core)
    offset = jnp.where(pair < 8, size * (1 - 2 * (pair % 2)), jnp.where(pair == 8, both, single))
    return offset, (parity + core) % 2


def exchange_kernel(
    part,
    states_hbm,
    sproj_hbm,
    sout_hbm,
    cproj_hbm,
    cout_hbm,
    gains,
    ctx_out,
    w_out,
    mixed_out,
    states_v,
    sproj_v,
    cproj_v,
    sw,
    x0,
    x2,
    kvbuf,
    far_send,
    far_recv,
    gathered,
    sums,
    sums_recv,
    mixed_v,
    normed,
    qbuf,
    ctxbuf,
    own_bits,
    partner_bits,
    in_sem,
    loc_sem,
    own_sem,
    send_sem,
    recv_sem,
    c_send,
    c_recv,
):
    me = lax.axis_index("owner")
    my_h = lax.axis_index("helper")
    core = me % 2
    chip = me // 2
    my_x = chip % X
    my_z = chip // X

    def chip_at(dz, dx):
        return (((my_z + dz + Z) % Z) * 2 * X + ((my_x + dx + X) % X) * 2 + core, my_h)

    def helper_at(step):
        return (me, (my_h + step) % HELPERS)

    sibling = (me + 1 - 2 * core, my_h)
    north, south, east, west = chip_at(1, 0), chip_at(-1, 0), chip_at(0, 1), chip_at(0, -1)
    far = chip_at(4, 0)
    greeted = [north, south, east, west, chip_at(0, 2), far, sibling]
    greeted += [helper_at(step) for step in range(1, HELPERS)]
    barrier = pltpu.get_barrier_semaphore()
    for device in greeted:
        pl.semaphore_signal(barrier, inc=1, device_id=device, device_id_type=MESH)

    loads = [
        pltpu.make_async_copy(states_hbm, states_v, in_sem.at[0]),
        pltpu.make_async_copy(cproj_hbm, cproj_v, in_sem.at[1]),
        pltpu.make_async_copy(sproj_hbm, sproj_v, in_sem.at[2]),
        pltpu.make_async_copy(sout_hbm, sw.at[pl.ds(PAD, COLS)], in_sem.at[3]),
        pltpu.make_async_copy(cout_hbm, w_out.at[0], in_sem.at[4]),
    ]
    for load in loads:
        load.start()

    copies = {}

    def send(name, source, landing, device, when=None, seen=None):
        number = len(copies)

        def describe(place):
            return pltpu.make_async_remote_copy(
                src_ref=source,
                dst_ref=place,
                send_sem=send_sem.at[number],
                recv_sem=recv_sem.at[number],
                device_id=device,
                device_id_type=MESH,
            )

        copies[name] = (functools.partial(describe, landing), functools.partial(describe, seen or landing), when)
        if when is None:
            describe(landing).start()
        else:
            pl.when(when)(lambda: describe(landing).start())

    def arrived(*names):
        for name in names:
            _, seen, when = copies[name]
            if when is None:
                seen().wait_recv()
            else:
                pl.when(when)(lambda: seen().wait_recv())

    mine, other = gathered.at[0], gathered.at[1]

    def share(row, col, when=None):
        send(f"s{row}{col}", mine.at[row, col], other.at[row, col], sibling, when)

    loads[0].wait()
    as_float = states_v[...].reshape(IMAGES * PATCHES, D).astype(F32)
    row_mean = jnp.mean(as_float, -1, keepdims=True)
    centred = as_float - row_mean
    row_var = jnp.mean(centred * centred, -1, keepdims=True)
    scaled = centred * lax.rsqrt(row_var + 1e-05)
    x2[...] = (scaled * gains[2:3, :]).astype(BF16)
    x0[...] = (scaled * gains[0:1, :]).astype(BF16)

    loads[1].wait()
    key_rows = dot_nt(x2[...], cproj_v[1])
    value_rows = dot_nt(x2[...], cproj_v[2])
    tiles = pair_tiles(key_rows, value_rows)
    for parity in range(2):
        for h in range(HEADS):
            for image in range(IMAGES):
                kvbuf[parity, image, :, 128 * h : 128 * (h + 1)] = tiles[parity][h][
                    PATCHES * image : PATCHES * (image + 1)
                ]

    opposite = 2 * ((me + OWNERS // 2) % OWNERS)
    far_bit = jnp.int32(0)
    for s in range(SLOTS):
        p = part[1, s]
        far_bit = jnp.where(jnp.logical_and(p >= opposite, p <= opposite + 1), 1, far_bit)
    far_send[...] = kvbuf[0, far_bit]

    pl.semaphore_wait(barrier, len(greeted))

    own = kvbuf.at[core]
    send("x+0", own.at[0], mine.at[2, 3, 0], east)
    send("x-1", own.at[1], mine.at[2, 1, 1], west)
    send("z+", own, mine.at[1, 0], north)
    send("z-", own, mine.at[3, 0], south)
    send("x+1", own.at[1], mine.at[2, 3, 1], east)
    send("x-0", own.at[0], mine.at[2, 1, 0], west)
    send("s20", own, other.at[2, 0], sibling)

    def weight_piece(x):
        return pl.ds(pl.multiple_of(x * WPIECE, 16), WPIECE)

    def weight_half(c):
        return pl.ds(pl.multiple_of(c * (D // 2), 128), D // 2)

    for step in range(1, HELPERS):
        send(
            f"w{step}",
            cout_hbm.at[weight_piece(my_x), weight_half(core)],
            w_out.at[HELPERS - step, weight_piece(my_x), weight_half(core)],
            helper_at(step),
        )

    sw[0:PAD] = jnp.zeros((PAD, D), BF16)
    sw[PAD + COLS :] = jnp.zeros((PAD, D), BF16)
    loads[2].wait()
    sq = dot_nt(x0[...], sproj_v[0]) * HEAD ** (-0.5)
    sk = dot_nt(x0[...], sproj_v[1])
    sv = dot_nt(x0[...], sproj_v[2])
    q_tiles = pair_tiles(sq, None)
    kv_tiles = pair_tiles(sk, sv)
    pieces = [slice(PATCHES * image, PATCHES * (image + 1)) for image in range(IMAGES)]
    contexts = head_contexts(
        [
            (q_tiles[image][h][pieces[image]], kv_tiles[image][h][pieces[image]])
            for image in range(IMAGES)
            for h in range(HEADS)
        ]
    )
    joined = join_contexts(contexts[:HEADS], contexts[HEADS:])
    loads[3].wait()
    sums[0] = dot(jnp.concatenate(joined[0:2], axis=1), sw[PAD:]).astype(BF16)
    sums[1] = dot(jnp.concatenate(joined[1:3], axis=1), sw[0 : PAD + COLS]).astype(BF16)

    def rows_of(step):
        return pl.ds(pl.multiple_of(((my_h + step) % HELPERS) * ROWS, ROWS), ROWS)

    for step in range(1, HELPERS):
        send(f"p{step}", sums.at[:, rows_of(step)], sums_recv.at[step - 1], helper_at(step))

    over_x, over_z = pl.ds(0, ACROSS), pl.ds(ACROSS, PATCHES - ACROSS)
    arrived("x+0")
    send("x++", mine.at[2, 3, 0], mine.at[2, 2, 0], east)
    arrived("x-1")
    send("x--", mine.at[2, 1, 1], mine.at[2, 2, 1], west)
    arrived("x+1")
    send("x+z+", mine.at[2, 3, :, over_z], mine.at[1, 3, :, over_z], north)
    send("x+z-", mine.at[2, 3, :, over_z], mine.at[3, 3, :, over_z], south)
    arrived("x-0")
    send("x-z+", mine.at[2, 1, :, over_z], mine.at[1, 1, :, over_z], north)
    send("x-z-", mine.at[2, 1, :, over_z], mine.at[3, 1, :, over_z], south)
    arrived("z+")
    send("z+x+", mine.at[1, 0, :, over_x], mine.at[1, 3, :, over_x], east)
    send("z+x-", mine.at[1, 0, :, over_x], mine.at[1, 1, :, over_x], west)
    arrived("z-")
    send("z-x+", mine.at[3, 0, :, over_x], mine.at[3, 3, :, over_x], east)
    send("z-x-", mine.at[3, 0, :, over_x], mine.at[3, 1, :, over_x], west)
    send("far", far_send, far_recv, far)
    share(2, 3)
    share(2, 1)
    share(1, 0)
    share(3, 0)

    arrived("p1", "p2", "p3")
    mixed_v[...] = (
        states_v[:, rows_of(0)].astype(F32)
        + sums[:, rows_of(0)].astype(F32)
        + sums_recv[0].astype(F32)
        + sums_recv[1].astype(F32)
        + sums_recv[2].astype(F32)
    )
    mixed = mixed_v[...]
    row_mean = jnp.mean(mixed, -1, keepdims=True)
    centred = mixed - row_mean
    row_var = jnp.mean(centred * centred, -1, keepdims=True)
    normed[0] = (centred * lax.rsqrt(row_var + 1e-05) * gains[1:2, :].reshape(1, 1, D)).astype(BF16)
    for step in range(1, HELPERS):
        send(f"n{step}", normed.at[0], normed.at[HELPERS - step], helper_at(step))
    mixed_copy = pltpu.make_async_copy(mixed_v, mixed_out, loc_sem.at[0])
    mixed_copy.start()

    arrived("w1", "w2", "w3")
    for step in (1, 3, 2):
        send(
            f"wx{step}",
            w_out.at[pl.ds(1, 3), weight_piece(my_x), weight_half(core)],
            w_out.at[pl.ds(1, 3), weight_piece(my_x), weight_half(core)],
            chip_at(0, step),
            seen=w_out.at[pl.ds(1, 3), weight_piece((my_x + X - step) % X), weight_half(core)],
        )

    @pl.loop(0, SLOTS)
    def _(m):
        offset, layer = slot_owner(m // 2, m % 2, core)
        target = 2 * ((chip + offset + OWNERS // 2) % (OWNERS // 2)) + (layer + core) % 2
        target = 2 * jnp.where(m == SLOTS - 1, (me + OWNERS // 2) % OWNERS, target)
        code = jnp.int32(0)
        for image in range(IMAGES):
            for s in range(SLOTS):
                past = part[image, s] - target
                hit = jnp.logical_and(past >= 0, past <= 1)
                code = jnp.where(hit, 2 * image + past, code)
        own_bits[m] = code // 2
        partner_bits[m] = code % 2

    arrived("x--", "x++")
    send("x2z+", mine.at[2, 2, :, over_z], mine.at[1, 2, :, over_z], north)
    send("x2z-", mine.at[2, 2, :, over_z], mine.at[3, 2, :, over_z], south)
    share(2, 2)
    arrived("z+x+")
    send("z+x++", mine.at[1, 3, :, over_x], mine.at[1, 2, :, over_x], east)
    arrived("z-x-")
    send("z-x--", mine.at[3, 1, :, over_x], mine.at[3, 2, :, over_x], west)
    first_x, last_x = my_x == 0, my_x == X - 1
    arrived("x+z+")
    send("c0", mine.at[1, 3], mine.at[0, 3], north, first_x)
    share(1, 3)
    arrived("x-z-")
    send("c3", mine.at[3, 1], mine.at[4, 1], south, last_x)
    share(3, 1)

    arrived("n1", "n2", "n3")
    queries = dot_nt(normed[...].reshape(IMAGES * PATCHES, D), cproj_v[0]) * HEAD ** (-0.5)
    q_tiles = pair_tiles(queries, None)
    for parity in range(2):
        for h in range(HEADS):
            for step in range(HELPERS):
                for image in range(IMAGES):
                    start = ROWS * (IMAGES * step + image)
                    qbuf[parity, image, h, rows_of(step)] = q_tiles[parity][h][start : start + ROWS]

    def context_copy(pair, step):
        return pltpu.make_async_remote_copy(
            src_ref=ctxbuf.at[pair, rows_of(step)],
            dst_ref=ctx_out.at[HELPERS - step, pair],
            send_sem=c_send.at[pair, step - 1],
            recv_sem=c_recv.at[pair, step - 1],
            device_id=helper_at(step),
            device_id_type=MESH,
        )

    def own_copy(pair):
        return pltpu.make_async_copy(
            ctxbuf.at[pair, rows_of(0)], ctx_out.at[0, pair], own_sem.at[pair]
        )

    def slot_tiles(pair, parity):
        m = 2 * pair + parity
        offset, layer = slot_owner(pair, parity, core)
        col = (offset + 2 * X) % X
        row = (my_x + offset + 2 * X) // X
        image, which = own_bits[m], partner_bits[m]
        kv = jnp.where(
            which == 1, gathered[layer, row, col, 1], gathered[layer, row, col, 0]
        )
        return [
            (qbuf[parity, image, h], kv[:, 128 * h : 128 * (h + 1)]) for h in range(HEADS)
        ]

    def finish_pair(pair, even, odd):
        for t, tile in enumerate(join_contexts(even, odd)):
            ctxbuf[pair, :, 128 * t : 128 * (t + 1)] = tile
        for step in (2, 1, 3):
            context_copy(pair, step).start()
        own_copy(pair).start()

    def work_pairs(first, last):
        @pl.loop(first, last)
        def _(pair):
            contexts = head_contexts(slot_tiles(pair, 0) + slot_tiles(pair, 1))
            finish_pair(pair, contexts[:HEADS], contexts[HEADS:])

    arrived("s10", "s30")
    work_pairs(0, 2)
    arrived("z+x-", "x-z+")
    share(1, 1)
    arrived("z-x+", "x+z-")
    share(3, 3)
    arrived("s23", "s21", "s13", "s31", "s11", "s33")
    work_pairs(2, 6)
    arrived("z+x++", "x2z+")
    share(1, 2)
    arrived("z-x--", "x2z-")
    share(3, 2)
    arrived("wx1", "wx2", "wx3")
    send(
        "ws",
        w_out.at[pl.ds(1, 3), :, weight_half(core)],
        w_out.at[pl.ds(1, 3), :, weight_half(core)],
        sibling,
        seen=w_out.at[pl.ds(1, 3), :, weight_half(1 - core)],
    )
    arrived("s22", "s12", "s32")
    work_pairs(6, 8)
    arrived("c0", "c3")
    share(0, 3, first_x)
    share(4, 1, last_x)
    arrived("s20", "s03", "s41")
    work_pairs(8, 10)
    arrived("far")
    far_tiles = [
        (qbuf[0, own_bits[SLOTS - 1], h], far_recv[:, 128 * h : 128 * (h + 1)]) for h in range(HEADS)
    ]
    finish_pair(PAIRS - 1, head_contexts(far_tiles), None)

    arrived("ws")
    loads[4].wait()
    mixed_copy.wait()
    for sent, _, when in copies.values():
        if when is None:
            sent().wait_send()
        else:
            pl.when(when)(lambda: sent().wait_send())

    @pl.loop(0, PAIRS)
    def _(pair):
        for step in range(1, HELPERS):
            context_copy(pair, step).wait()
        own_copy(pair).wait()


def place_kernel(
    part, ctx_hbm, w_hbm, mixed, out, ctx, w, result, blank, places, ctx_sem, w_sem, out_sem, blank_sem
):
    me = lax.axis_index("owner")
    load_w = pltpu.make_async_copy(w_hbm, w.at[:, pl.ds(PAD, COLS)], w_sem)
    load_ctx = pltpu.make_async_copy(ctx_hbm, ctx, ctx_sem)
    load_w.start()
    load_ctx.start()
    w[:, 0:PAD] = jnp.zeros((HELPERS, PAD, D), BF16)
    w[:, PAD + COLS :] = jnp.zeros((HELPERS, PAD, D), BF16)
    blank[...] = jnp.zeros((ROWS, D), BF16)

    def blank_copy(image, slot):
        return pltpu.make_async_copy(blank, out.at[image, slot], blank_sem.at[image, slot])

    for image in range(IMAGES):

        @pl.loop(0, SLOTS)
        def _(slot):
            p = part[image, slot]
            owner = lax.div(jnp.maximum(p, 0), 2)
            parity = owner % 2
            chips = OWNERS // 2
            offset = (owner // 2 - me // 2 + chips + chips // 2) % chips - chips // 2
            size = jnp.abs(offset)
            group = jnp.where(size == 4, 0, jnp.where(size == 1, 1, jnp.where(size == 3, 2, 3)))
            pair = 2 * group + jnp.where(offset < 0, 1, 0)
            pair = jnp.where(size == 5, jnp.where(offset == 10 * (me % 2) - 5, 8, 9), pair)
            pair = jnp.where(size == 0, 9, pair)
            index = jnp.where(size == chips // 2, SLOTS - 1, 2 * pair + parity)
            index = jnp.clip(index, 0, SLOTS - 1)

            @pl.when(p >= 0)
            def _():
                places[index] = image * SLOTS + slot

            @pl.when(p < 0)
            def _():
                blank_copy(image, slot).start()

    load_w.wait()
    load_ctx.wait()

    def out_copy(index):
        place = places[index]
        return pltpu.make_async_copy(
            result.at[index],
            out.at[lax.div(place, SLOTS), lax.rem(place, SLOTS)],
            out_sem.at[index],
        )

    for first, count in ((0, 6), (6, 5)):
        for parity in range(2):
            start, weight_rows = (0, slice(PAD, None)) if parity == 0 else (128, slice(0, 256))
            lhs = jnp.concatenate(
                [
                    ctx[h, first : first + count, :, start : start + 256].reshape(count * ROWS, 256)
                    for h in range(HELPERS)
                ],
                axis=1,
            )
            rhs = jnp.concatenate([w[h, weight_rows] for h in range(HELPERS)], axis=0)
            terms = dot(lhs, rhs)
            for n in range(count):
                index = 2 * (first + n) + parity
                if index < SLOTS:
                    image = lax.div(places[index], SLOTS)
                    result[index] = (terms[ROWS * n : ROWS * (n + 1)] + mixed[image]).astype(BF16)
                    out_copy(index).start()

    @pl.loop(0, SLOTS)
    def _(index):
        out_copy(index).wait()

    for image in range(IMAGES):

        @pl.loop(0, SLOTS)
        def _(slot):
            @pl.when(part[image, slot] < 0)
            def _():
                blank_copy(image, slot).wait()


def local(states, partners, self_proj, self_out, cross_proj, cross_out, gains):
    any_spec = pl.BlockSpec(memory_space=pl.ANY)
    smem = pl.BlockSpec(memory_space=pltpu.SMEM)
    vmem = pl.BlockSpec(memory_space=pltpu.VMEM)
    dma = pltpu.SemaphoreType.DMA
    ctx, weight, mixed = pl.pallas_call(
        exchange_kernel,
        out_shape=(
            jax.ShapeDtypeStruct((HELPERS, PAIRS, ROWS, LANES), BF16),
            jax.ShapeDtypeStruct((HELPERS, COLS, D), BF16),
            jax.ShapeDtypeStruct((IMAGES, ROWS, D), F32),
        ),
        in_specs=[smem, any_spec, any_spec, any_spec, any_spec, any_spec, vmem],
        out_specs=(any_spec, any_spec, any_spec),
        scratch_shapes=[
            pltpu.VMEM((IMAGES, PATCHES, D), BF16),
            pltpu.VMEM((3, COLS, D), BF16),
            pltpu.VMEM((3, COLS, D), BF16),
            pltpu.VMEM((COLS + 2 * PAD, D), BF16),
            pltpu.VMEM((IMAGES * PATCHES, D), BF16),
            pltpu.VMEM((IMAGES * PATCHES, D), BF16),
            pltpu.VMEM((2, IMAGES, PATCHES, LANES), BF16),
            pltpu.VMEM((PATCHES, LANES), BF16),
            pltpu.VMEM((PATCHES, LANES), BF16),
            pltpu.VMEM((2, 5, X, IMAGES, PATCHES, LANES), BF16),
            pltpu.VMEM((IMAGES, PATCHES, D), BF16),
            pltpu.VMEM((HELPERS - 1, IMAGES, ROWS, D), BF16),
            pltpu.VMEM((IMAGES, ROWS, D), F32),
            pltpu.VMEM((HELPERS, IMAGES, ROWS, D), BF16),
            pltpu.VMEM((2, IMAGES, HEADS, PATCHES, 2 * HEAD), BF16),
            pltpu.VMEM((PAIRS, PATCHES, LANES), BF16),
            pltpu.SMEM((SLOTS,), jnp.int32),
            pltpu.SMEM((SLOTS,), jnp.int32),
            dma((5,)),
            dma((1,)),
            dma((PAIRS,)),
            dma((COPIES,)),
            dma((COPIES,)),
            dma((PAIRS, 3)),
            dma((PAIRS, 3)),
        ],
        compiler_params=pltpu.CompilerParams(
            collective_id=0, has_side_effects=True, vmem_limit_bytes=VMEM_LIMIT
        ),
        name="exchange",
    )(
        partners,
        states,
        jnp.swapaxes(self_proj, 1, 2),
        self_out,
        jnp.swapaxes(cross_proj, 1, 2),
        cross_out,
        gains,
    )
    return pl.pallas_call(
        place_kernel,
        out_shape=jax.ShapeDtypeStruct((IMAGES, SLOTS, ROWS, D), BF16),
        in_specs=[smem, any_spec, any_spec, vmem],
        out_specs=any_spec,
        scratch_shapes=[
            pltpu.VMEM((HELPERS, PAIRS, ROWS, LANES), BF16),
            pltpu.VMEM((HELPERS, COLS + 2 * PAD, D), BF16),
            pltpu.VMEM((SLOTS, ROWS, D), BF16),
            pltpu.VMEM((ROWS, D), BF16),
            pltpu.SMEM((SLOTS,), jnp.int32),
            dma,
            dma,
            dma((SLOTS,)),
            dma((IMAGES, SLOTS)),
        ],
        compiler_params=pltpu.CompilerParams(vmem_limit_bytes=VMEM_LIMIT),
        name="place",
    )(partners, ctx, weight, mixed)


def solution(mesh):
    return jax.shard_map(
        local,
        mesh=mesh,
        in_specs=(
            P("owner", None, None),
            P("owner", None),
            P(None, None, "helper"),
            P("helper", None),
            P(None, None, "helper"),
            P("helper", None),
            P(),
        ),
        out_specs=P("owner", None, "helper", None),
        check_vma=False,
    )
```

```python
import functools

import jax
import jax.numpy as jnp
from jax import lax
from jax.experimental import pallas as pl
from jax.experimental.pallas import tpu as pltpu
from jax.sharding import PartitionSpec as P

MESH = pl.DeviceIdType.MESH
BF16 = jnp.bfloat16
F32 = jnp.float32

OWNERS = 64
HELPERS = 4
IMAGES = 2
PATCHES = 128
ROWS = PATCHES // HELPERS
D = 768
HEAD = 64
HEADS = 3
COLS = HEADS * HEAD
SLOTS = 21
X, Z = 4, 8
PAIRS = 11
ACROSS = 80
WPIECE = COLS // X
LANES = 2 * COLS
PAD = 64
COPIES = 64
VMEM_LIMIT = 56 * 1024 * 1024


def dot(a, b):
    return jnp.dot(a, b, preferred_element_type=F32)


def dot_nt(a, b):
    return lax.dot_general(a, b, (((1,), (1,)), ((), ())), preferred_element_type=F32)


def pair_tiles(first, second):
    zero = jnp.zeros((first.shape[0], HEAD), F32)
    f = [first[:, HEAD * h : HEAD * (h + 1)] for h in range(HEADS)]
    s = [zero] * HEADS if second is None else [second[:, HEAD * h : HEAD * (h + 1)] for h in range(HEADS)]
    tiles = []
    for parity in range(2):
        row = []
        for h in range(HEADS):
            ordered = (s[h], f[h]) if (h + parity) % 2 == 0 else (f[h], s[h])
            row.append(jnp.concatenate(ordered, axis=1).astype(BF16))
        tiles.append(row)
    return tiles


def head_contexts(tiles):
    scores = [dot_nt(q, kv) for q, kv in tiles]
    weights = [jnp.exp(s - jnp.max(s, axis=1, keepdims=True)) for s in scores]
    totals = [jnp.sum(w, axis=1, keepdims=True) for w in weights]
    return [
        dot(w.astype(BF16), kv) * (1.0 / t) for w, t, (_, kv) in zip(weights, totals, tiles)
    ]


def join_contexts(even, odd):
    low = lax.broadcasted_iota(jnp.int32, (PATCHES, 2 * HEAD), 1) < HEAD
    if odd is None:
        odd = [even[0], even[1], even[0]]
    return (
        jnp.where(low, even[0], even[1]).astype(BF16),
        jnp.where(low, even[2], odd[0]).astype(BF16),
        jnp.where(low, odd[1], odd[2]).astype(BF16),
    )


def slot_owner(pair, parity, core):
    group = pair // 2
    size = jnp.where(group == 0, 4, jnp.where(group == 1, 1, jnp.where(group == 2, 3, 2)))
    both = 10 * core - 5
    single = jnp.where(parity == 0, 5 * (1 - core), -5 * core)
    offset = jnp.where(pair < 8, size * (1 - 2 * (pair % 2)), jnp.where(pair == 8, both, single))
    return offset, (parity + core) % 2


def pair_at(n, x, core):
    first, last = x == 0, x == X - 1

    def pick(at_first, inside, at_last):
        return jnp.where(first, at_first, jnp.where(last, at_last, inside))

    low = x < X // 2
    eighth = pick(9 - core, 8, 8 + core)
    choices = [
        0,
        1,
        pick(2, 2, 3),
        pick(4, 3, 5),
        pick(3, 4, 2),
        pick(5, 5, 4),
        jnp.where(low, 6, 7),
        eighth,
        jnp.where(low, 7, 6),
        17 - eighth,
    ]
    pair = jnp.int32(0)
    for step, choice in enumerate(choices):
        pair = jnp.where(n == step, choice, pair)
    return pair


def exchange_kernel(
    part,
    states_hbm,
    sproj_hbm,
    sout_hbm,
    cproj_hbm,
    cout_hbm,
    gains,
    y_out,
    states_v,
    sproj_v,
    cproj_v,
    sw,
    x0,
    x2,
    kvbuf,
    far_send,
    far_recv,
    gathered,
    sums,
    sums_recv,
    mixed_v,
    normed,
    qbuf,
    ctxbuf,
    ctx_recv,
    w_all,
    y,
    own_bits,
    partner_bits,
    in_sem,
    y_sem,
    token_sem,
    send_sem,
    recv_sem,
    c_send,
    c_recv,
):
    me = lax.axis_index("owner")
    my_h = lax.axis_index("helper")
    core = me % 2
    chip = me // 2
    my_x = chip % X
    my_z = chip // X

    def chip_at(dz, dx):
        return (((my_z + dz + Z) % Z) * 2 * X + ((my_x + dx + X) % X) * 2 + core, my_h)

    def helper_at(step):
        return (me, (my_h + step) % HELPERS)

    sibling = (me + 1 - 2 * core, my_h)
    north, south, east, west = chip_at(1, 0), chip_at(-1, 0), chip_at(0, 1), chip_at(0, -1)
    far = chip_at(4, 0)
    greeted = [north, south, east, west, chip_at(0, 2), sibling]
    greeted += [helper_at(step) for step in range(1, HELPERS)]
    barrier = pltpu.get_barrier_semaphore()
    for device in greeted:
        pl.semaphore_signal(barrier, inc=1, device_id=device, device_id_type=MESH)

    loads = [
        pltpu.make_async_copy(states_hbm, states_v, in_sem.at[0]),
        pltpu.make_async_copy(cproj_hbm, cproj_v, in_sem.at[1]),
        pltpu.make_async_copy(sproj_hbm, sproj_v, in_sem.at[2]),
        pltpu.make_async_copy(sout_hbm, sw.at[pl.ds(PAD, COLS)], in_sem.at[3]),
        pltpu.make_async_copy(cout_hbm, w_all.at[0, pl.ds(PAD, COLS)], in_sem.at[4]),
    ]
    for load in loads:
        load.start()

    copies = {}

    def send(name, source, landing, device, when=None, seen=None):
        number = len(copies)

        def describe(place):
            return pltpu.make_async_remote_copy(
                src_ref=source,
                dst_ref=place,
                send_sem=send_sem.at[number],
                recv_sem=recv_sem.at[number],
                device_id=device,
                device_id_type=MESH,
            )

        copies[name] = (functools.partial(describe, landing), functools.partial(describe, seen or landing), when)
        if when is None:
            describe(landing).start()
        else:
            pl.when(when)(lambda: describe(landing).start())

    def arrived(*names):
        for name in names:
            _, seen, when = copies[name]
            if when is None:
                seen().wait_recv()
            else:
                pl.when(when)(lambda: seen().wait_recv())

    def token(n):
        if n > 1:
            pl.semaphore_wait(token_sem.at[n - 2], 2)
        if n < 4:
            for device in (north, south):
                pl.semaphore_signal(token_sem.at[n - 1], inc=1, device_id=device, device_id_type=MESH)

    mine, other = gathered.at[0], gathered.at[1]

    def share(row, col, when=None):
        send(f"s{row}{col}", mine.at[row, col], other.at[row, col], sibling, when)

    loads[0].wait()
    as_float = states_v[...].reshape(IMAGES * PATCHES, D).astype(F32)
    row_mean = jnp.mean(as_float, -1, keepdims=True)
    centred = as_float - row_mean
    row_var = jnp.mean(centred * centred, -1, keepdims=True)
    scaled = centred * lax.rsqrt(row_var + 1e-05)
    x2[...] = (scaled * gains[2:3, :]).astype(BF16)
    x0[...] = (scaled * gains[0:1, :]).astype(BF16)

    loads[1].wait()
    key_rows = dot_nt(x2[...], cproj_v[1])
    value_rows = dot_nt(x2[...], cproj_v[2])
    tiles = pair_tiles(key_rows, value_rows)
    for parity in range(2):
        for h in range(HEADS):
            for image in range(IMAGES):
                kvbuf[parity, image, :, 128 * h : 128 * (h + 1)] = tiles[parity][h][
                    PATCHES * image : PATCHES * (image + 1)
                ]

    opposite = 2 * ((me + OWNERS // 2) % OWNERS)
    far_bit = jnp.int32(0)
    for s in range(SLOTS):
        p = part[1, s]
        far_bit = jnp.where(jnp.logical_and(p >= opposite, p <= opposite + 1), 1, far_bit)
    far_send[...] = kvbuf[0, far_bit]

    pl.semaphore_wait(barrier, len(greeted))

    own = kvbuf.at[core]
    send("x+0", own.at[0], mine.at[2, 3, 0], east)
    send("x-1", own.at[1], mine.at[2, 1, 1], west)
    send("z+", own, mine.at[1, 0], north)
    send("z-", own, mine.at[3, 0], south)
    send("x+1", own.at[1], mine.at[2, 3, 1], east)
    send("x-0", own.at[0], mine.at[2, 1, 0], west)
    send("s20", own, other.at[2, 0], sibling)

    token(1)

    def weight_piece(x):
        return pl.ds(pl.multiple_of(x * WPIECE, 16), WPIECE)

    def weight_rows(x):
        return pl.ds(pl.multiple_of(PAD + x * WPIECE, 16), WPIECE)

    def weight_half(c):
        return pl.ds(pl.multiple_of(c * (D // 2), 128), D // 2)

    sw[0:PAD] = jnp.zeros((PAD, D), BF16)
    sw[PAD + COLS :] = jnp.zeros((PAD, D), BF16)
    w_all[:, 0:PAD] = jnp.zeros((HELPERS, PAD, D), BF16)
    w_all[:, PAD + COLS :] = jnp.zeros((HELPERS, PAD, D), BF16)
    loads[2].wait()
    sq = dot_nt(x0[...], sproj_v[0]) * HEAD ** (-0.5)
    sk = dot_nt(x0[...], sproj_v[1])
    sv = dot_nt(x0[...], sproj_v[2])
    q_tiles = pair_tiles(sq, None)
    kv_tiles = pair_tiles(sk, sv)
    def rows_of(step):
        return pl.ds(pl.multiple_of(((my_h + step) % HELPERS) * ROWS, ROWS), ROWS)

    loads[3].wait()
    for image in range(IMAGES):
        piece = slice(PATCHES * image, PATCHES * (image + 1))
        contexts = head_contexts(
            [(q_tiles[image][h][piece], kv_tiles[image][h][piece]) for h in range(HEADS)]
        )
        if image == 0:
            joined = join_contexts(contexts, None)[0:2]
            sums[0] = dot(jnp.concatenate(joined, axis=1), sw[PAD:]).astype(BF16)
        else:
            joined = join_contexts([contexts[1], contexts[0], contexts[1]], contexts)[1:3]
            sums[1] = dot(jnp.concatenate(joined, axis=1), sw[0 : PAD + COLS]).astype(BF16)
        for step in range(1, HELPERS):
            send(
                f"p{step}{image}",
                sums.at[image, rows_of(step)],
                sums_recv.at[step - 1, image],
                helper_at(step),
            )

    for step in range(1, HELPERS):
        send(
            f"w{step}",
            cout_hbm.at[weight_piece(my_x), weight_half(core)],
            w_all.at[HELPERS - step, weight_rows(my_x), weight_half(core)],
            helper_at(step),
        )

    over_x, over_z = pl.ds(0, ACROSS), pl.ds(ACROSS, PATCHES - ACROSS)
    arrived("x+0")
    token(2)
    send("x++", mine.at[2, 3, 0], mine.at[2, 2, 0], east)
    arrived("x-1")
    send("x--", mine.at[2, 1, 1], mine.at[2, 2, 1], west)
    arrived("x+1")
    send("x+z+", mine.at[2, 3, :, over_z], mine.at[1, 3, :, over_z], north)
    send("x+z-", mine.at[2, 3, :, over_z], mine.at[3, 3, :, over_z], south)
    arrived("x-0")
    send("x-z+", mine.at[2, 1, :, over_z], mine.at[1, 1, :, over_z], north)
    send("x-z-", mine.at[2, 1, :, over_z], mine.at[3, 1, :, over_z], south)
    arrived("z+")
    send("z+x+", mine.at[1, 0, :, over_x], mine.at[1, 3, :, over_x], east)
    send("z+x-", mine.at[1, 0, :, over_x], mine.at[1, 1, :, over_x], west)
    arrived("z-")
    send("z-x+", mine.at[3, 0, :, over_x], mine.at[3, 3, :, over_x], east)
    send("z-x-", mine.at[3, 0, :, over_x], mine.at[3, 1, :, over_x], west)
    token(3)
    share(2, 3)
    share(2, 1)
    share(1, 0)
    share(3, 0)

    for image in range(IMAGES):
        arrived(*[f"p{step}{image}" for step in range(1, HELPERS)])
        mixed = (
            states_v[image, rows_of(0)].astype(F32)
            + sums[image, rows_of(0)].astype(F32)
            + sums_recv[0, image].astype(F32)
            + sums_recv[1, image].astype(F32)
            + sums_recv[2, image].astype(F32)
        )
        mixed_v[image] = mixed
        row_mean = jnp.mean(mixed, -1, keepdims=True)
        centred = mixed - row_mean
        row_var = jnp.mean(centred * centred, -1, keepdims=True)
        normed[0, image] = (centred * lax.rsqrt(row_var + 1e-05) * gains[1:2, :]).astype(BF16)
        for step in range(1, HELPERS):
            send(
                f"n{step}{image}",
                normed.at[0, image],
                normed.at[HELPERS - step, image],
                helper_at(step),
            )

    token(4)
    send("far", far_send, far_recv, far)

    @pl.loop(0, SLOTS)
    def _(m):
        offset, layer = slot_owner(m // 2, m % 2, core)
        target = 2 * ((chip + offset + OWNERS // 2) % (OWNERS // 2)) + (layer + core) % 2
        target = 2 * jnp.where(m == SLOTS - 1, (me + OWNERS // 2) % OWNERS, target)
        code = jnp.int32(0)
        for image in range(IMAGES):
            for s in range(SLOTS):
                past = part[image, s] - target
                hit = jnp.logical_and(past >= 0, past <= 1)
                code = jnp.where(hit, 2 * image + past, code)
        own_bits[m] = code // 2
        partner_bits[m] = code % 2

    arrived("x--", "x++")
    send("x2z+", mine.at[2, 2, :, over_z], mine.at[1, 2, :, over_z], north)
    send("x2z-", mine.at[2, 2, :, over_z], mine.at[3, 2, :, over_z], south)
    share(2, 2)
    arrived("z+x+")
    send("z+x++", mine.at[1, 3, :, over_x], mine.at[1, 2, :, over_x], east)
    arrived("z-x-")
    send("z-x--", mine.at[3, 1, :, over_x], mine.at[3, 2, :, over_x], west)
    first_x, last_x = my_x == 0, my_x == X - 1
    arrived("x+z+")
    send("c0", mine.at[1, 3], mine.at[0, 3], north, first_x)
    share(1, 3)
    arrived("x-z-")
    send("c3", mine.at[3, 1], mine.at[4, 1], south, last_x)
    share(3, 1)

    arrived("w1", "w2", "w3")
    for step in (1, 3, 2):
        send(
            f"wx{step}",
            w_all.at[pl.ds(1, 3), weight_rows(my_x), weight_half(core)],
            w_all.at[pl.ds(1, 3), weight_rows(my_x), weight_half(core)],
            chip_at(0, step),
            seen=w_all.at[pl.ds(1, 3), weight_rows((my_x + X - step) % X), weight_half(core)],
        )

    for image in range(IMAGES):
        arrived(*[f"n{step}{image}" for step in range(1, HELPERS)])
        rows = normed[:, image].reshape(PATCHES, D)
        q_tiles = pair_tiles(dot_nt(rows, cproj_v[0]) * HEAD ** (-0.5), None)
        for parity in range(2):
            for h in range(HEADS):
                for step in range(HELPERS):
                    qbuf[parity, image, h, rows_of(step)] = q_tiles[parity][h][
                        ROWS * step : ROWS * (step + 1)
                    ]

    def context_copy(n, step):
        return pltpu.make_async_remote_copy(
            src_ref=ctxbuf.at[n, rows_of(step)],
            dst_ref=ctx_recv.at[HELPERS - 1 - step, n],
            send_sem=c_send.at[n, step - 1],
            recv_sem=c_recv.at[n, step - 1],
            device_id=helper_at(step),
            device_id_type=MESH,
        )

    def slot_tiles(pair, parity):
        m = 2 * pair + parity
        offset, layer = slot_owner(pair, parity, core)
        col = (offset + 2 * X) % X
        row = (my_x + offset + 2 * X) // X
        image, which = own_bits[m], partner_bits[m]
        kv = jnp.where(
            which == 1, gathered[layer, row, col, 1], gathered[layer, row, col, 0]
        )
        return [
            (qbuf[parity, image, h], kv[:, 128 * h : 128 * (h + 1)]) for h in range(HEADS)
        ]

    def finish_pair(n, even, odd):
        for t, tile in enumerate(join_contexts(even, odd)):
            ctxbuf[n, :, 128 * t : 128 * (t + 1)] = tile
        for step in (2, 1, 3):
            context_copy(n, step).start()

    def work_pairs(first, last):
        @pl.loop(first, last)
        def _(n):
            pair = pair_at(n, my_x, core)
            contexts = head_contexts(slot_tiles(pair, 0) + slot_tiles(pair, 1))
            finish_pair(n, contexts[:HEADS], contexts[HEADS:])

    def y_copy(first, count):
        return pltpu.make_async_copy(
            y.at[pl.ds(2 * first, 2 * count)], y_out.at[pl.ds(2 * first, 2 * count)], y_sem.at[first]
        )

    def project(first, count):
        @pl.loop(first, first + count)
        def _(n):
            for step in range(1, HELPERS):
                context_copy(n, step).wait()

        for parity in range(2):
            start, weight_rows = (0, slice(PAD, None)) if parity == 0 else (128, slice(0, 256))
            cut = slice(start, start + 256)
            blocks = [ctxbuf[first : first + count, rows_of(0), cut]]
            blocks += [ctx_recv[rel - 1, first : first + count, :, cut] for rel in range(1, HELPERS)]
            lhs = jnp.concatenate([block.reshape(count * ROWS, 256) for block in blocks], axis=1)
            rhs = jnp.concatenate([w_all[rel, weight_rows] for rel in range(HELPERS)], axis=0)
            terms = dot(lhs, rhs)
            for i in range(count):
                n = first + i
                last = n == PAIRS - 1
                m = SLOTS - 1 if last else 2 * pair_at(n, my_x, core) + parity
                y[2 * n + parity] = (
                    terms[ROWS * i : ROWS * (i + 1)] + mixed_v[own_bits[m]]
                ).astype(BF16)
        y_copy(first, count).start()

    arrived("s10", "s30", "s23", "s21")
    work_pairs(0, 4)
    arrived("z+x-", "x-z+")
    share(1, 1)
    arrived("z-x+", "x+z-")
    share(3, 3)
    arrived("s22", "s13", "s31", "s11", "s33", "s20")
    work_pairs(4, 8)
    arrived("far")
    far_tiles = [
        (qbuf[0, own_bits[SLOTS - 1], h], far_recv[:, 128 * h : 128 * (h + 1)]) for h in range(HEADS)
    ]
    finish_pair(PAIRS - 1, head_contexts(far_tiles), None)
    arrived("wx1", "wx2", "wx3")
    send(
        "ws",
        w_all.at[pl.ds(1, 3), pl.ds(PAD, COLS), weight_half(core)],
        w_all.at[pl.ds(1, 3), pl.ds(PAD, COLS), weight_half(core)],
        sibling,
        seen=w_all.at[pl.ds(1, 3), pl.ds(PAD, COLS), weight_half(1 - core)],
    )
    arrived("z+x++", "x2z+")
    share(1, 2)
    arrived("z-x--", "x2z-")
    share(3, 2)
    arrived("c0", "c3")
    share(0, 3, first_x)
    share(4, 1, last_x)
    arrived("ws")
    loads[4].wait()
    project(0, 4)
    arrived("s12", "s32", "s03", "s41")
    work_pairs(8, 10)
    project(4, 4)
    project(8, 3)

    for sent, _, when in copies.values():
        if when is None:
            sent().wait_send()
        else:
            pl.when(when)(lambda: sent().wait_send())

    y_copy(0, 4).wait()
    y_copy(4, 4).wait()
    y_copy(8, 3).wait()


def place_kernel(part, y, out, blank, steps, out_sem):
    me = lax.axis_index("owner")
    blank[...] = jnp.zeros((ROWS, D), BF16)

    @pl.loop(0, PAIRS - 1)
    def _(n):
        steps[pair_at(n, (me // 2) % X, me % 2)] = n

    def result_copy(index, image, slot):
        return pltpu.make_async_copy(y.at[index], out.at[image, slot], out_sem.at[image, slot])

    def blank_copy(image, slot):
        return pltpu.make_async_copy(blank, out.at[image, slot], out_sem.at[image, slot])

    for image in range(IMAGES):

        @pl.loop(0, SLOTS)
        def _(slot):
            p = part[image, slot]
            owner = lax.div(jnp.maximum(p, 0), 2)
            parity = owner % 2
            chips = OWNERS // 2
            offset = (owner // 2 - me // 2 + chips + chips // 2) % chips - chips // 2
            size = jnp.abs(offset)
            group = jnp.where(size == 4, 0, jnp.where(size == 1, 1, jnp.where(size == 3, 2, 3)))
            pair = 2 * group + jnp.where(offset < 0, 1, 0)
            pair = jnp.where(size == 5, jnp.where(offset == 10 * (me % 2) - 5, 8, 9), pair)
            pair = jnp.where(size == 0, 9, pair)
            index = 2 * steps[jnp.minimum(pair, 9)] + parity
            index = jnp.where(size == chips // 2, SLOTS - 1, index)

            @pl.when(p >= 0)
            def _():
                result_copy(index, image, slot).start()

            @pl.when(p < 0)
            def _():
                blank_copy(image, slot).start()

    for image in range(IMAGES):

        @pl.loop(0, SLOTS)
        def _(slot):
            blank_copy(image, slot).wait()


def local(states, partners, self_proj, self_out, cross_proj, cross_out, gains):
    any_spec = pl.BlockSpec(memory_space=pl.ANY)
    smem = pl.BlockSpec(memory_space=pltpu.SMEM)
    vmem = pl.BlockSpec(memory_space=pltpu.VMEM)
    dma = pltpu.SemaphoreType.DMA
    y = pl.pallas_call(
        exchange_kernel,
        out_shape=jax.ShapeDtypeStruct((2 * PAIRS, ROWS, D), BF16),
        in_specs=[smem, any_spec, any_spec, any_spec, any_spec, any_spec, vmem],
        out_specs=any_spec,
        scratch_shapes=[
            pltpu.VMEM((IMAGES, PATCHES, D), BF16),
            pltpu.VMEM((3, COLS, D), BF16),
            pltpu.VMEM((3, COLS, D), BF16),
            pltpu.VMEM((COLS + 2 * PAD, D), BF16),
            pltpu.VMEM((IMAGES * PATCHES, D), BF16),
            pltpu.VMEM((IMAGES * PATCHES, D), BF16),
            pltpu.VMEM((2, IMAGES, PATCHES, LANES), BF16),
            pltpu.VMEM((PATCHES, LANES), BF16),
            pltpu.VMEM((PATCHES, LANES), BF16),
            pltpu.VMEM((2, 5, X, IMAGES, PATCHES, LANES), BF16),
            pltpu.VMEM((IMAGES, PATCHES, D), BF16),
            pltpu.VMEM((HELPERS - 1, IMAGES, ROWS, D), BF16),
            pltpu.VMEM((IMAGES, ROWS, D), F32),
            pltpu.VMEM((HELPERS, IMAGES, ROWS, D), BF16),
            pltpu.VMEM((2, IMAGES, HEADS, PATCHES, 2 * HEAD), BF16),
            pltpu.VMEM((PAIRS, PATCHES, LANES), BF16),
            pltpu.VMEM((HELPERS - 1, PAIRS, ROWS, LANES), BF16),
            pltpu.VMEM((HELPERS, COLS + 2 * PAD, D), BF16),
            pltpu.VMEM((2 * PAIRS, ROWS, D), BF16),
            pltpu.SMEM((SLOTS,), jnp.int32),
            pltpu.SMEM((SLOTS,), jnp.int32),
            dma((5,)),
            dma((PAIRS,)),
            pltpu.SemaphoreType.REGULAR((3,)),
            dma((COPIES,)),
            dma((COPIES,)),
            dma((PAIRS, 3)),
            dma((PAIRS, 3)),
        ],
        compiler_params=pltpu.CompilerParams(
            collective_id=0, has_side_effects=True, vmem_limit_bytes=VMEM_LIMIT
        ),
        name="exchange",
    )(
        partners,
        states,
        jnp.swapaxes(self_proj, 1, 2),
        self_out,
        jnp.swapaxes(cross_proj, 1, 2),
        cross_out,
        gains,
    )
    return pl.pallas_call(
        place_kernel,
        out_shape=jax.ShapeDtypeStruct((IMAGES, SLOTS, ROWS, D), BF16),
        in_specs=[smem, vmem],
        out_specs=any_spec,
        scratch_shapes=[
            pltpu.VMEM((ROWS, D), BF16),
            pltpu.SMEM((PAIRS,), jnp.int32),
            dma((IMAGES, SLOTS)),
        ],
        compiler_params=pltpu.CompilerParams(vmem_limit_bytes=VMEM_LIMIT),
        name="place",
    )(partners, y)


def solution(mesh):
    return jax.shard_map(
        local,
        mesh=mesh,
        in_specs=(
            P("owner", None, None),
            P("owner", None),
            P(None, None, "helper"),
            P("helper", None),
            P(None, None, "helper"),
            P("helper", None),
            P(),
        ),
        out_specs=P("owner", None, "helper", None),
        check_vma=False,
    )
```

```python
import functools

import jax
import jax.numpy as jnp
from jax import lax
from jax.experimental import pallas as pl
from jax.experimental.pallas import tpu as pltpu
from jax.sharding import PartitionSpec as P

MESH = pl.DeviceIdType.MESH
BF16 = jnp.bfloat16
F32 = jnp.float32

OWNERS = 64
HELPERS = 4
IMAGES = 2
PATCHES = 128
ROWS = PATCHES // HELPERS
D = 768
HEAD = 64
HEADS = 3
COLS = HEADS * HEAD
SLOTS = 21
X, Z = 4, 8
PAIRS = 11
ACROSS = 80
WPIECE = COLS // X
LANES = 2 * COLS
PAD = 64
COPIES = 64
VMEM_LIMIT = 56 * 1024 * 1024


def dot(a, b):
    return jnp.dot(a, b, preferred_element_type=F32)


def dot_nt(a, b):
    return lax.dot_general(a, b, (((1,), (1,)), ((), ())), preferred_element_type=F32)


def pair_tiles(first, second):
    zero = jnp.zeros((first.shape[0], HEAD), F32)
    f = [first[:, HEAD * h : HEAD * (h + 1)] for h in range(HEADS)]
    s = [zero] * HEADS if second is None else [second[:, HEAD * h : HEAD * (h + 1)] for h in range(HEADS)]
    tiles = []
    for parity in range(2):
        row = []
        for h in range(HEADS):
            ordered = (s[h], f[h]) if (h + parity) % 2 == 0 else (f[h], s[h])
            row.append(jnp.concatenate(ordered, axis=1).astype(BF16))
        tiles.append(row)
    return tiles


def head_contexts(tiles):
    scores = [dot_nt(q, kv) for q, kv in tiles]
    weights = [jnp.exp(s - jnp.max(s, axis=1, keepdims=True)) for s in scores]
    totals = [jnp.sum(w, axis=1, keepdims=True) for w in weights]
    return [
        dot(w.astype(BF16), kv) * (1.0 / t) for w, t, (_, kv) in zip(weights, totals, tiles)
    ]


def join_contexts(even, odd):
    low = lax.broadcasted_iota(jnp.int32, (PATCHES, 2 * HEAD), 1) < HEAD
    if odd is None:
        odd = [even[0], even[1], even[0]]
    return (
        jnp.where(low, even[0], even[1]).astype(BF16),
        jnp.where(low, even[2], odd[0]).astype(BF16),
        jnp.where(low, odd[1], odd[2]).astype(BF16),
    )


def slot_owner(pair, parity, core):
    group = pair // 2
    size = jnp.where(group == 0, 4, jnp.where(group == 1, 1, jnp.where(group == 2, 3, 2)))
    both = 10 * core - 5
    single = jnp.where(parity == 0, 5 * (1 - core), -5 * core)
    offset = jnp.where(pair < 8, size * (1 - 2 * (pair % 2)), jnp.where(pair == 8, both, single))
    return offset, (parity + core) % 2


def pair_at(n, x, core):
    first, last = x == 0, x == X - 1

    def pick(at_first, inside, at_last):
        return jnp.where(first, at_first, jnp.where(last, at_last, inside))

    low = x < X // 2
    eighth = pick(9 - core, 8, 8 + core)
    choices = [
        0,
        1,
        pick(2, 2, 3),
        pick(4, 3, 5),
        pick(3, 4, 2),
        pick(5, 5, 4),
        jnp.where(low, 6, 7),
        eighth,
        jnp.where(low, 7, 6),
        17 - eighth,
    ]
    pair = jnp.int32(0)
    for step, choice in enumerate(choices):
        pair = jnp.where(n == step, choice, pair)
    return pair


def exchange_kernel(
    part,
    states_hbm,
    sproj_hbm,
    sout_hbm,
    cproj_hbm,
    cout_hbm,
    gains,
    y_out,
    states_v,
    sproj_v,
    cproj_v,
    sw,
    x0,
    x2,
    kvbuf,
    far_send,
    far_recv,
    gathered,
    sums,
    sums_recv,
    mixed_v,
    normed,
    qbuf,
    ctxbuf,
    ctx_recv,
    w_all,
    y,
    own_bits,
    partner_bits,
    in_sem,
    y_sem,
    token_sem,
    send_sem,
    recv_sem,
    c_send,
    c_recv,
):
    me = lax.axis_index("owner")
    my_h = lax.axis_index("helper")
    core = me % 2
    chip = me // 2
    my_x = chip % X
    my_z = chip // X

    def chip_at(dz, dx):
        return (((my_z + dz + Z) % Z) * 2 * X + ((my_x + dx + X) % X) * 2 + core, my_h)

    def helper_at(step):
        return (me, (my_h + step) % HELPERS)

    sibling = (me + 1 - 2 * core, my_h)
    north, south, east, west = chip_at(1, 0), chip_at(-1, 0), chip_at(0, 1), chip_at(0, -1)
    far = chip_at(4, 0)
    greeted = [north, south, east, west, chip_at(0, 2), sibling]
    greeted += [helper_at(step) for step in range(1, HELPERS)]
    barrier = pltpu.get_barrier_semaphore()
    for device in greeted:
        pl.semaphore_signal(barrier, inc=1, device_id=device, device_id_type=MESH)

    loads = [
        pltpu.make_async_copy(states_hbm, states_v, in_sem.at[0]),
        pltpu.make_async_copy(cproj_hbm, cproj_v, in_sem.at[1]),
        pltpu.make_async_copy(sproj_hbm, sproj_v, in_sem.at[2]),
        pltpu.make_async_copy(sout_hbm, sw.at[pl.ds(PAD, COLS)], in_sem.at[3]),
        pltpu.make_async_copy(cout_hbm, w_all.at[0, pl.ds(PAD, COLS)], in_sem.at[4]),
    ]
    for load in loads:
        load.start()

    copies = {}

    def send(name, source, landing, device, when=None, seen=None):
        number = len(copies)

        def describe(place):
            return pltpu.make_async_remote_copy(
                src_ref=source,
                dst_ref=place,
                send_sem=send_sem.at[number],
                recv_sem=recv_sem.at[number],
                device_id=device,
                device_id_type=MESH,
            )

        copies[name] = (functools.partial(describe, landing), functools.partial(describe, seen or landing), when)
        if when is None:
            describe(landing).start()
        else:
            pl.when(when)(lambda: describe(landing).start())

    def arrived(*names):
        for name in names:
            _, seen, when = copies[name]
            if when is None:
                seen().wait_recv()
            else:
                pl.when(when)(lambda: seen().wait_recv())

    def token(n):
        if n > 1:
            pl.semaphore_wait(token_sem.at[n - 2], 2)
        if n < 4:
            for device in (north, south):
                pl.semaphore_signal(token_sem.at[n - 1], inc=1, device_id=device, device_id_type=MESH)

    mine, other = gathered.at[0], gathered.at[1]

    def share(row, col, when=None):
        send(f"s{row}{col}", mine.at[row, col], other.at[row, col], sibling, when)

    loads[0].wait()
    as_float = states_v[...].reshape(IMAGES * PATCHES, D).astype(F32)
    row_mean = jnp.mean(as_float, -1, keepdims=True)
    centred = as_float - row_mean
    row_var = jnp.mean(centred * centred, -1, keepdims=True)
    scaled = centred * lax.rsqrt(row_var + 1e-05)
    x2[...] = (scaled * gains[2:3, :]).astype(BF16)
    x0[...] = (scaled * gains[0:1, :]).astype(BF16)

    loads[1].wait()
    key_rows = dot_nt(x2[...], cproj_v[1])
    value_rows = dot_nt(x2[...], cproj_v[2])
    tiles = pair_tiles(key_rows, value_rows)
    for parity in range(2):
        for h in range(HEADS):
            for image in range(IMAGES):
                kvbuf[parity, image, :, 128 * h : 128 * (h + 1)] = tiles[parity][h][
                    PATCHES * image : PATCHES * (image + 1)
                ]

    opposite = 2 * ((me + OWNERS // 2) % OWNERS)
    far_bit = jnp.int32(0)
    for s in range(SLOTS):
        p = part[1, s]
        far_bit = jnp.where(jnp.logical_and(p >= opposite, p <= opposite + 1), 1, far_bit)
    far_send[...] = kvbuf[0, far_bit]

    pl.semaphore_wait(barrier, len(greeted))

    own = kvbuf.at[core]
    send("x+0", own.at[0], mine.at[2, 3, 0], east)
    send("x-1", own.at[1], mine.at[2, 1, 1], west)
    send("z+", own, mine.at[1, 0], north)
    send("z-", own, mine.at[3, 0], south)
    send("x+1", own.at[1], mine.at[2, 3, 1], east)
    send("x-0", own.at[0], mine.at[2, 1, 0], west)
    send("s20", own, other.at[2, 0], sibling)

    token(1)

    def weight_piece(x):
        return pl.ds(pl.multiple_of(x * WPIECE, 16), WPIECE)

    def weight_rows(x):
        return pl.ds(pl.multiple_of(PAD + x * WPIECE, 16), WPIECE)

    def weight_half(c):
        return pl.ds(pl.multiple_of(c * (D // 2), 128), D // 2)

    sw[0:PAD] = jnp.zeros((PAD, D), BF16)
    sw[PAD + COLS :] = jnp.zeros((PAD, D), BF16)
    w_all[:, 0:PAD] = jnp.zeros((HELPERS, PAD, D), BF16)
    w_all[:, PAD + COLS :] = jnp.zeros((HELPERS, PAD, D), BF16)
    loads[2].wait()
    sq = dot_nt(x0[...], sproj_v[0]) * HEAD ** (-0.5)
    sk = dot_nt(x0[...], sproj_v[1])
    sv = dot_nt(x0[...], sproj_v[2])
    q_tiles = pair_tiles(sq, None)
    kv_tiles = pair_tiles(sk, sv)
    def rows_of(step):
        return pl.ds(pl.multiple_of(((my_h + step) % HELPERS) * ROWS, ROWS), ROWS)

    token(2)
    loads[3].wait()
    for image in range(IMAGES):
        piece = slice(PATCHES * image, PATCHES * (image + 1))
        contexts = head_contexts(
            [(q_tiles[image][h][piece], kv_tiles[image][h][piece]) for h in range(HEADS)]
        )
        if image == 0:
            joined = join_contexts(contexts, None)[0:2]
            sums[0] = dot(jnp.concatenate(joined, axis=1), sw[PAD:]).astype(BF16)
        else:
            joined = join_contexts([contexts[1], contexts[0], contexts[1]], contexts)[1:3]
            sums[1] = dot(jnp.concatenate(joined, axis=1), sw[0 : PAD + COLS]).astype(BF16)
        for step in range(1, HELPERS):
            send(
                f"p{step}{image}",
                sums.at[image, rows_of(step)],
                sums_recv.at[step - 1, image],
                helper_at(step),
            )

    for step in range(1, HELPERS):
        send(
            f"w{step}",
            cout_hbm.at[weight_piece(my_x), weight_half(core)],
            w_all.at[HELPERS - step, weight_rows(my_x), weight_half(core)],
            helper_at(step),
        )

    over_x, over_z = pl.ds(0, ACROSS), pl.ds(ACROSS, PATCHES - ACROSS)
    token(3)
    arrived("x+0")
    send("x++", mine.at[2, 3, 0], mine.at[2, 2, 0], east)
    arrived("x-1")
    send("x--", mine.at[2, 1, 1], mine.at[2, 2, 1], west)
    arrived("x+1")
    send("x+z+", mine.at[2, 3, :, over_z], mine.at[1, 3, :, over_z], north)
    send("x+z-", mine.at[2, 3, :, over_z], mine.at[3, 3, :, over_z], south)
    arrived("x-0")
    send("x-z+", mine.at[2, 1, :, over_z], mine.at[1, 1, :, over_z], north)
    send("x-z-", mine.at[2, 1, :, over_z], mine.at[3, 1, :, over_z], south)
    token(4)
    send("far", far_send, far_recv, far)
    arrived("z+")
    send("z+x+", mine.at[1, 0, :, over_x], mine.at[1, 3, :, over_x], east)
    send("z+x-", mine.at[1, 0, :, over_x], mine.at[1, 1, :, over_x], west)
    arrived("z-")
    send("z-x+", mine.at[3, 0, :, over_x], mine.at[3, 3, :, over_x], east)
    send("z-x-", mine.at[3, 0, :, over_x], mine.at[3, 1, :, over_x], west)
    share(2, 3)
    share(2, 1)
    share(1, 0)
    share(3, 0)

    for image in range(IMAGES):
        arrived(*[f"p{step}{image}" for step in range(1, HELPERS)])
        mixed = (
            states_v[image, rows_of(0)].astype(F32)
            + sums[image, rows_of(0)].astype(F32)
            + sums_recv[0, image].astype(F32)
            + sums_recv[1, image].astype(F32)
            + sums_recv[2, image].astype(F32)
        )
        mixed_v[image] = mixed
        row_mean = jnp.mean(mixed, -1, keepdims=True)
        centred = mixed - row_mean
        row_var = jnp.mean(centred * centred, -1, keepdims=True)
        normed[0, image] = (centred * lax.rsqrt(row_var + 1e-05) * gains[1:2, :]).astype(BF16)
        for step in range(1, HELPERS):
            send(
                f"n{step}{image}",
                normed.at[0, image],
                normed.at[HELPERS - step, image],
                helper_at(step),
            )

    arrived("w1", "w2", "w3")
    for step in (1, 3, 2):
        send(
            f"wx{step}",
            w_all.at[pl.ds(1, 3), weight_rows(my_x), weight_half(core)],
            w_all.at[pl.ds(1, 3), weight_rows(my_x), weight_half(core)],
            chip_at(0, step),
            seen=w_all.at[pl.ds(1, 3), weight_rows((my_x + X - step) % X), weight_half(core)],
        )

    arrived("x--", "x++")
    send("x2z+", mine.at[2, 2, :, over_z], mine.at[1, 2, :, over_z], north)
    send("x2z-", mine.at[2, 2, :, over_z], mine.at[3, 2, :, over_z], south)
    share(2, 2)
    first_x, last_x = my_x == 0, my_x == X - 1
    arrived("x+z+")
    send("c0z", mine.at[1, 3, :, over_z], mine.at[0, 3, :, over_z], north, first_x)
    arrived("x-z-")
    send("c3z", mine.at[3, 1, :, over_z], mine.at[4, 1, :, over_z], south, last_x)
    @pl.loop(0, SLOTS)
    def _(m):
        offset, layer = slot_owner(m // 2, m % 2, core)
        target = 2 * ((chip + offset + OWNERS // 2) % (OWNERS // 2)) + (layer + core) % 2
        target = 2 * jnp.where(m == SLOTS - 1, (me + OWNERS // 2) % OWNERS, target)
        code = jnp.int32(0)
        for image in range(IMAGES):
            for s in range(SLOTS):
                past = part[image, s] - target
                hit = jnp.logical_and(past >= 0, past <= 1)
                code = jnp.where(hit, 2 * image + past, code)
        own_bits[m] = code // 2
        partner_bits[m] = code % 2

    arrived("z+x+")
    send("z+x++", mine.at[1, 3, :, over_x], mine.at[1, 2, :, over_x], east)
    send("c0x", mine.at[1, 3, :, over_x], mine.at[0, 3, :, over_x], north, first_x)
    arrived("z-x-")
    send("z-x--", mine.at[3, 1, :, over_x], mine.at[3, 2, :, over_x], west)
    send("c3x", mine.at[3, 1, :, over_x], mine.at[4, 1, :, over_x], south, last_x)
    share(1, 3)
    share(3, 1)
    for image in range(IMAGES):
        arrived(*[f"n{step}{image}" for step in range(1, HELPERS)])
        rows = normed[:, image].reshape(PATCHES, D)
        q_tiles = pair_tiles(dot_nt(rows, cproj_v[0]) * HEAD ** (-0.5), None)
        for parity in range(2):
            for h in range(HEADS):
                for step in range(HELPERS):
                    qbuf[parity, image, h, rows_of(step)] = q_tiles[parity][h][
                        ROWS * step : ROWS * (step + 1)
                    ]

    def context_copy(n, step):
        return pltpu.make_async_remote_copy(
            src_ref=ctxbuf.at[n, rows_of(step)],
            dst_ref=ctx_recv.at[HELPERS - 1 - step, n],
            send_sem=c_send.at[n, step - 1],
            recv_sem=c_recv.at[n, step - 1],
            device_id=helper_at(step),
            device_id_type=MESH,
        )

    def slot_tiles(pair, parity):
        m = 2 * pair + parity
        offset, layer = slot_owner(pair, parity, core)
        col = (offset + 2 * X) % X
        row = (my_x + offset + 2 * X) // X
        image, which = own_bits[m], partner_bits[m]
        kv = jnp.where(
            which == 1, gathered[layer, row, col, 1], gathered[layer, row, col, 0]
        )
        return [
            (qbuf[parity, image, h], kv[:, 128 * h : 128 * (h + 1)]) for h in range(HEADS)
        ]

    def finish_pair(n, even, odd):
        for t, tile in enumerate(join_contexts(even, odd)):
            ctxbuf[n, :, 128 * t : 128 * (t + 1)] = tile
        for step in (2, 1, 3):
            context_copy(n, step).start()

    def work_pairs(first, last):
        @pl.loop(first, last)
        def _(n):
            pair = pair_at(n, my_x, core)
            contexts = head_contexts(slot_tiles(pair, 0) + slot_tiles(pair, 1))
            finish_pair(n, contexts[:HEADS], contexts[HEADS:])

    def y_copy(first, count):
        return pltpu.make_async_copy(
            y.at[pl.ds(2 * first, 2 * count)], y_out.at[pl.ds(2 * first, 2 * count)], y_sem.at[first]
        )

    def project(first, count):
        @pl.loop(first, first + count)
        def _(n):
            for step in range(1, HELPERS):
                context_copy(n, step).wait()

        for parity in range(2):
            start, weight_rows = (0, slice(PAD, None)) if parity == 0 else (128, slice(0, 256))
            cut = slice(start, start + 256)
            blocks = [ctxbuf[first : first + count, rows_of(0), cut]]
            blocks += [ctx_recv[rel - 1, first : first + count, :, cut] for rel in range(1, HELPERS)]
            lhs = jnp.concatenate([block.reshape(count * ROWS, 256) for block in blocks], axis=1)
            rhs = jnp.concatenate([w_all[rel, weight_rows] for rel in range(HELPERS)], axis=0)
            terms = dot(lhs, rhs)
            for i in range(count):
                n = first + i
                last = n == PAIRS - 1
                m = SLOTS - 1 if last else 2 * pair_at(n, my_x, core) + parity
                y[2 * n + parity] = (
                    terms[ROWS * i : ROWS * (i + 1)] + mixed_v[own_bits[m]]
                ).astype(BF16)
        y_copy(first, count).start()

    arrived("s10", "s30", "s23", "s21")
    work_pairs(0, 4)
    arrived("z+x-", "x-z+")
    share(1, 1)
    arrived("z-x+", "x+z-")
    share(3, 3)
    arrived("s22", "s13", "s31", "s11", "s33", "s20")
    work_pairs(4, 8)
    arrived("far")
    far_tiles = [
        (qbuf[0, own_bits[SLOTS - 1], h], far_recv[:, 128 * h : 128 * (h + 1)]) for h in range(HEADS)
    ]
    finish_pair(PAIRS - 1, head_contexts(far_tiles), None)
    arrived("wx1", "wx2", "wx3")
    send(
        "ws",
        w_all.at[pl.ds(1, 3), pl.ds(PAD, COLS), weight_half(core)],
        w_all.at[pl.ds(1, 3), pl.ds(PAD, COLS), weight_half(core)],
        sibling,
        seen=w_all.at[pl.ds(1, 3), pl.ds(PAD, COLS), weight_half(1 - core)],
    )
    arrived("z+x++", "x2z+")
    share(1, 2)
    arrived("z-x--", "x2z-")
    share(3, 2)
    arrived("c0z", "c3z", "c0x", "c3x")
    share(0, 3, first_x)
    share(4, 1, last_x)
    arrived("ws")
    loads[4].wait()
    project(0, 4)
    arrived("s12", "s32", "s03", "s41")
    work_pairs(8, 10)
    project(4, 4)
    project(8, 3)

    for sent, _, when in copies.values():
        if when is None:
            sent().wait_send()
        else:
            pl.when(when)(lambda: sent().wait_send())

    y_copy(0, 4).wait()
    y_copy(4, 4).wait()
    y_copy(8, 3).wait()


def place_kernel(part, y, out, blank, steps, out_sem):
    me = lax.axis_index("owner")
    blank[...] = jnp.zeros((ROWS, D), BF16)

    @pl.loop(0, PAIRS - 1)
    def _(n):
        steps[pair_at(n, (me // 2) % X, me % 2)] = n

    def result_copy(index, image, slot):
        return pltpu.make_async_copy(y.at[index], out.at[image, slot], out_sem.at[image, slot])

    def blank_copy(image, slot):
        return pltpu.make_async_copy(blank, out.at[image, slot], out_sem.at[image, slot])

    for image in range(IMAGES):

        @pl.loop(0, SLOTS)
        def _(slot):
            p = part[image, slot]
            owner = lax.div(jnp.maximum(p, 0), 2)
            parity = owner % 2
            chips = OWNERS // 2
            offset = (owner // 2 - me // 2 + chips + chips // 2) % chips - chips // 2
            size = jnp.abs(offset)
            group = jnp.where(size == 4, 0, jnp.where(size == 1, 1, jnp.where(size == 3, 2, 3)))
            pair = 2 * group + jnp.where(offset < 0, 1, 0)
            pair = jnp.where(size == 5, jnp.where(offset == 10 * (me % 2) - 5, 8, 9), pair)
            pair = jnp.where(size == 0, 9, pair)
            index = 2 * steps[jnp.minimum(pair, 9)] + parity
            index = jnp.where(size == chips // 2, SLOTS - 1, index)

            @pl.when(p >= 0)
            def _():
                result_copy(index, image, slot).start()

            @pl.when(p < 0)
            def _():
                blank_copy(image, slot).start()

    for image in range(IMAGES):

        @pl.loop(0, SLOTS)
        def _(slot):
            blank_copy(image, slot).wait()


def local(states, partners, self_proj, self_out, cross_proj, cross_out, gains):
    any_spec = pl.BlockSpec(memory_space=pl.ANY)
    smem = pl.BlockSpec(memory_space=pltpu.SMEM)
    vmem = pl.BlockSpec(memory_space=pltpu.VMEM)
    dma = pltpu.SemaphoreType.DMA
    y = pl.pallas_call(
        exchange_kernel,
        out_shape=jax.ShapeDtypeStruct((2 * PAIRS, ROWS, D), BF16),
        in_specs=[smem, any_spec, any_spec, any_spec, any_spec, any_spec, vmem],
        out_specs=any_spec,
        scratch_shapes=[
            pltpu.VMEM((IMAGES, PATCHES, D), BF16),
            pltpu.VMEM((3, COLS, D), BF16),
            pltpu.VMEM((3, COLS, D), BF16),
            pltpu.VMEM((COLS + 2 * PAD, D), BF16),
            pltpu.VMEM((IMAGES * PATCHES, D), BF16),
            pltpu.VMEM((IMAGES * PATCHES, D), BF16),
            pltpu.VMEM((2, IMAGES, PATCHES, LANES), BF16),
            pltpu.VMEM((PATCHES, LANES), BF16),
            pltpu.VMEM((PATCHES, LANES), BF16),
            pltpu.VMEM((2, 5, X, IMAGES, PATCHES, LANES), BF16),
            pltpu.VMEM((IMAGES, PATCHES, D), BF16),
            pltpu.VMEM((HELPERS - 1, IMAGES, ROWS, D), BF16),
            pltpu.VMEM((IMAGES, ROWS, D), F32),
            pltpu.VMEM((HELPERS, IMAGES, ROWS, D), BF16),
            pltpu.VMEM((2, IMAGES, HEADS, PATCHES, 2 * HEAD), BF16),
            pltpu.VMEM((PAIRS, PATCHES, LANES), BF16),
            pltpu.VMEM((HELPERS - 1, PAIRS, ROWS, LANES), BF16),
            pltpu.VMEM((HELPERS, COLS + 2 * PAD, D), BF16),
            pltpu.VMEM((2 * PAIRS, ROWS, D), BF16),
            pltpu.SMEM((SLOTS,), jnp.int32),
            pltpu.SMEM((SLOTS,), jnp.int32),
            dma((5,)),
            dma((PAIRS,)),
            pltpu.SemaphoreType.REGULAR((3,)),
            dma((COPIES,)),
            dma((COPIES,)),
            dma((PAIRS, 3)),
            dma((PAIRS, 3)),
        ],
        compiler_params=pltpu.CompilerParams(
            collective_id=0, has_side_effects=True, vmem_limit_bytes=VMEM_LIMIT
        ),
        name="exchange",
    )(
        partners,
        states,
        jnp.swapaxes(self_proj, 1, 2),
        self_out,
        jnp.swapaxes(cross_proj, 1, 2),
        cross_out,
        gains,
    )
    return pl.pallas_call(
        place_kernel,
        out_shape=jax.ShapeDtypeStruct((IMAGES, SLOTS, ROWS, D), BF16),
        in_specs=[smem, vmem],
        out_specs=any_spec,
        scratch_shapes=[
            pltpu.VMEM((ROWS, D), BF16),
            pltpu.SMEM((PAIRS,), jnp.int32),
            dma((IMAGES, SLOTS)),
        ],
        compiler_params=pltpu.CompilerParams(vmem_limit_bytes=VMEM_LIMIT),
        name="place",
    )(partners, y)


def solution(mesh):
    return jax.shard_map(
        local,
        mesh=mesh,
        in_specs=(
            P("owner", None, None),
            P("owner", None),
            P(None, None, "helper"),
            P("helper", None),
            P(None, None, "helper"),
            P("helper", None),
            P(),
        ),
        out_specs=P("owner", None, "helper", None),
        check_vma=False,
    )
```

```python
import functools

import jax
import jax.numpy as jnp
from jax import lax
from jax.experimental import pallas as pl
from jax.experimental.pallas import tpu as pltpu
from jax.sharding import PartitionSpec as P

MESH = pl.DeviceIdType.MESH
BF16 = jnp.bfloat16
F32 = jnp.float32

OWNERS = 64
HELPERS = 4
IMAGES = 2
PATCHES = 128
ROWS = PATCHES // HELPERS
D = 768
HEAD = 64
HEADS = 3
COLS = HEADS * HEAD
SLOTS = 21
X, Z = 4, 8
PAIRS = 11
ACROSS = 80
WPIECE = COLS // X
LANES = 2 * COLS
PAD = 64
COPIES = 64
VMEM_LIMIT = 56 * 1024 * 1024


def dot(a, b):
    return jnp.dot(a, b, preferred_element_type=F32)


def dot_nt(a, b):
    return lax.dot_general(a, b, (((1,), (1,)), ((), ())), preferred_element_type=F32)


def pair_tiles(first, second):
    zero = jnp.zeros((first.shape[0], HEAD), F32)
    f = [first[:, HEAD * h : HEAD * (h + 1)] for h in range(HEADS)]
    s = [zero] * HEADS if second is None else [second[:, HEAD * h : HEAD * (h + 1)] for h in range(HEADS)]
    tiles = []
    for parity in range(2):
        row = []
        for h in range(HEADS):
            ordered = (s[h], f[h]) if (h + parity) % 2 == 0 else (f[h], s[h])
            row.append(jnp.concatenate(ordered, axis=1).astype(BF16))
        tiles.append(row)
    return tiles


def head_contexts(tiles):
    scores = [dot_nt(q, kv) for q, kv in tiles]
    weights = [jnp.exp(s - jnp.max(s, axis=1, keepdims=True)) for s in scores]
    totals = [jnp.sum(w, axis=1, keepdims=True) for w in weights]
    return [
        dot(w.astype(BF16), kv) * (1.0 / t) for w, t, (_, kv) in zip(weights, totals, tiles)
    ]


def join_contexts(even, odd):
    low = lax.broadcasted_iota(jnp.int32, (PATCHES, 2 * HEAD), 1) < HEAD
    if odd is None:
        odd = [even[0], even[1], even[0]]
    return (
        jnp.where(low, even[0], even[1]).astype(BF16),
        jnp.where(low, even[2], odd[0]).astype(BF16),
        jnp.where(low, odd[1], odd[2]).astype(BF16),
    )


def slot_owner(pair, parity, core):
    group = pair // 2
    size = jnp.where(group == 0, 4, jnp.where(group == 1, 1, jnp.where(group == 2, 3, 2)))
    both = 10 * core - 5
    single = jnp.where(parity == 0, 5 * (1 - core), -5 * core)
    offset = jnp.where(pair < 8, size * (1 - 2 * (pair % 2)), jnp.where(pair == 8, both, single))
    return offset, (parity + core) % 2


def pair_at(n, x, core):
    first, last = x == 0, x == X - 1

    def pick(at_first, inside, at_last):
        return jnp.where(first, at_first, jnp.where(last, at_last, inside))

    low = x < X // 2
    eighth = pick(9 - core, 8, 8 + core)
    choices = [
        0,
        1,
        pick(2, 2, 3),
        pick(4, 3, 5),
        pick(3, 4, 2),
        pick(5, 5, 4),
        jnp.where(low, 6, 7),
        eighth,
        jnp.where(low, 7, 6),
        17 - eighth,
    ]
    pair = jnp.int32(0)
    for step, choice in enumerate(choices):
        pair = jnp.where(n == step, choice, pair)
    return pair


def exchange_kernel(
    part,
    states_hbm,
    sproj_hbm,
    sout_hbm,
    cproj_hbm,
    cout_hbm,
    gains,
    y_out,
    states_v,
    sproj_v,
    cproj_v,
    sw,
    x0,
    x2,
    kvbuf,
    far_send,
    far_recv,
    gathered,
    sums,
    sums_recv,
    mixed_v,
    normed,
    qbuf,
    ctxbuf,
    ctx_recv,
    w_all,
    y,
    own_bits,
    partner_bits,
    in_sem,
    y_sem,
    token_sem,
    send_sem,
    recv_sem,
    c_send,
    c_recv,
):
    me = lax.axis_index("owner")
    my_h = lax.axis_index("helper")
    core = me % 2
    chip = me // 2
    my_x = chip % X
    my_z = chip // X

    def chip_at(dz, dx):
        return (((my_z + dz + Z) % Z) * 2 * X + ((my_x + dx + X) % X) * 2 + core, my_h)

    def helper_at(step):
        return (me, (my_h + step) % HELPERS)

    sibling = (me + 1 - 2 * core, my_h)
    north, south, east, west = chip_at(1, 0), chip_at(-1, 0), chip_at(0, 1), chip_at(0, -1)
    far = chip_at(4, 0)
    greeted = [north, south, east, west, chip_at(0, 2), sibling]
    greeted += [helper_at(step) for step in range(1, HELPERS)]
    barrier = pltpu.get_barrier_semaphore()
    for device in greeted:
        pl.semaphore_signal(barrier, inc=1, device_id=device, device_id_type=MESH)

    loads = [
        pltpu.make_async_copy(states_hbm, states_v, in_sem.at[0]),
        pltpu.make_async_copy(cproj_hbm, cproj_v, in_sem.at[1]),
        pltpu.make_async_copy(sproj_hbm, sproj_v, in_sem.at[2]),
        pltpu.make_async_copy(sout_hbm, sw.at[pl.ds(PAD, COLS)], in_sem.at[3]),
        pltpu.make_async_copy(cout_hbm, w_all.at[0, pl.ds(PAD, COLS)], in_sem.at[4]),
    ]
    for load in loads:
        load.start()

    copies = {}

    def send(name, source, landing, device, when=None, seen=None):
        number = len(copies)

        def describe(place):
            return pltpu.make_async_remote_copy(
                src_ref=source,
                dst_ref=place,
                send_sem=send_sem.at[number],
                recv_sem=recv_sem.at[number],
                device_id=device,
                device_id_type=MESH,
            )

        copies[name] = (functools.partial(describe, landing), functools.partial(describe, seen or landing), when)
        if when is None:
            describe(landing).start()
        else:
            pl.when(when)(lambda: describe(landing).start())

    def arrived(*names):
        for name in names:
            _, seen, when = copies[name]
            if when is None:
                seen().wait_recv()
            else:
                pl.when(when)(lambda: seen().wait_recv())

    def token(n):
        if n > 1:
            pl.semaphore_wait(token_sem.at[n - 2], 2)
        if n < 4:
            for device in (north, south):
                pl.semaphore_signal(token_sem.at[n - 1], inc=1, device_id=device, device_id_type=MESH)

    mine, other = gathered.at[0], gathered.at[1]

    def share(row, col, when=None):
        send(f"s{row}{col}", mine.at[row, col], other.at[row, col], sibling, when)

    loads[0].wait()
    as_float = states_v[...].reshape(IMAGES * PATCHES, D).astype(F32)
    row_mean = jnp.mean(as_float, -1, keepdims=True)
    centred = as_float - row_mean
    row_var = jnp.mean(centred * centred, -1, keepdims=True)
    scaled = centred * lax.rsqrt(row_var + 1e-05)
    x2[...] = (scaled * gains[2:3, :]).astype(BF16)
    x0[...] = (scaled * gains[0:1, :]).astype(BF16)

    loads[1].wait()
    key_rows = dot_nt(x2[...], cproj_v[1])
    value_rows = dot_nt(x2[...], cproj_v[2])
    tiles = pair_tiles(key_rows, value_rows)
    for parity in range(2):
        for h in range(HEADS):
            for image in range(IMAGES):
                kvbuf[parity, image, :, 128 * h : 128 * (h + 1)] = tiles[parity][h][
                    PATCHES * image : PATCHES * (image + 1)
                ]

    opposite = 2 * ((me + OWNERS // 2) % OWNERS)
    far_bit = jnp.int32(0)
    for s in range(SLOTS):
        p = part[1, s]
        far_bit = jnp.where(jnp.logical_and(p >= opposite, p <= opposite + 1), 1, far_bit)
    far_send[...] = kvbuf[0, far_bit]

    pl.semaphore_wait(barrier, len(greeted))

    own = kvbuf.at[core]
    send("x+0", own.at[0], mine.at[2, 3, 0], east)
    send("x-1", own.at[1], mine.at[2, 1, 1], west)
    send("z+", own, mine.at[1, 0], north)
    send("z-", own, mine.at[3, 0], south)
    send("x+1", own.at[1], mine.at[2, 3, 1], east)
    send("x-0", own.at[0], mine.at[2, 1, 0], west)
    send("s20", own, other.at[2, 0], sibling)

    token(1)

    def weight_piece(x):
        return pl.ds(pl.multiple_of(x * WPIECE, 16), WPIECE)

    def weight_rows(x):
        return pl.ds(pl.multiple_of(PAD + x * WPIECE, 16), WPIECE)

    def weight_half(c):
        return pl.ds(pl.multiple_of(c * (D // 2), 128), D // 2)

    sw[0:PAD] = jnp.zeros((PAD, D), BF16)
    sw[PAD + COLS :] = jnp.zeros((PAD, D), BF16)
    w_all[:, 0:PAD] = jnp.zeros((HELPERS, PAD, D), BF16)
    w_all[:, PAD + COLS :] = jnp.zeros((HELPERS, PAD, D), BF16)
    loads[2].wait()
    sq = dot_nt(x0[...], sproj_v[0]) * HEAD ** (-0.5)
    sk = dot_nt(x0[...], sproj_v[1])
    sv = dot_nt(x0[...], sproj_v[2])
    q_tiles = pair_tiles(sq, None)
    kv_tiles = pair_tiles(sk, sv)
    def rows_of(step):
        return pl.ds(pl.multiple_of(((my_h + step) % HELPERS) * ROWS, ROWS), ROWS)

    token(2)
    loads[3].wait()
    for image in range(IMAGES):
        piece = slice(PATCHES * image, PATCHES * (image + 1))
        contexts = head_contexts(
            [(q_tiles[image][h][piece], kv_tiles[image][h][piece]) for h in range(HEADS)]
        )
        if image == 0:
            joined = join_contexts(contexts, None)[0:2]
            sums[0] = dot(jnp.concatenate(joined, axis=1), sw[PAD:]).astype(BF16)
        else:
            joined = join_contexts([contexts[1], contexts[0], contexts[1]], contexts)[1:3]
            sums[1] = dot(jnp.concatenate(joined, axis=1), sw[0 : PAD + COLS]).astype(BF16)
        for step in range(1, HELPERS):
            send(
                f"p{step}{image}",
                sums.at[image, rows_of(step)],
                sums_recv.at[step - 1, image],
                helper_at(step),
            )

    for step in range(1, HELPERS):
        send(
            f"w{step}",
            cout_hbm.at[weight_piece(my_x), weight_half(core)],
            w_all.at[HELPERS - step, weight_rows(my_x), weight_half(core)],
            helper_at(step),
        )

    over_x, over_z = pl.ds(0, ACROSS), pl.ds(ACROSS, PATCHES - ACROSS)
    token(3)
    arrived("x+0")
    send("x++", mine.at[2, 3, 0], mine.at[2, 2, 0], east)
    arrived("x-1")
    send("x--", mine.at[2, 1, 1], mine.at[2, 2, 1], west)
    arrived("x+1")
    send("x+z+", mine.at[2, 3, :, over_z], mine.at[1, 3, :, over_z], north)
    send("x+z-", mine.at[2, 3, :, over_z], mine.at[3, 3, :, over_z], south)
    arrived("x-0")
    send("x-z+", mine.at[2, 1, :, over_z], mine.at[1, 1, :, over_z], north)
    send("x-z-", mine.at[2, 1, :, over_z], mine.at[3, 1, :, over_z], south)
    token(4)
    send("far", far_send, far_recv, far)
    arrived("z+")
    send("z+x+", mine.at[1, 0, :, over_x], mine.at[1, 3, :, over_x], east)
    send("z+x-", mine.at[1, 0, :, over_x], mine.at[1, 1, :, over_x], west)
    arrived("z-")
    send("z-x+", mine.at[3, 0, :, over_x], mine.at[3, 3, :, over_x], east)
    send("z-x-", mine.at[3, 0, :, over_x], mine.at[3, 1, :, over_x], west)
    share(2, 3)
    share(2, 1)
    share(1, 0)
    share(3, 0)

    for image in range(IMAGES):
        arrived(*[f"p{step}{image}" for step in range(1, HELPERS)])
        mixed = (
            states_v[image, rows_of(0)].astype(F32)
            + sums[image, rows_of(0)].astype(F32)
            + sums_recv[0, image].astype(F32)
            + sums_recv[1, image].astype(F32)
            + sums_recv[2, image].astype(F32)
        )
        mixed_v[image] = mixed
        row_mean = jnp.mean(mixed, -1, keepdims=True)
        centred = mixed - row_mean
        row_var = jnp.mean(centred * centred, -1, keepdims=True)
        normed[0, image] = (centred * lax.rsqrt(row_var + 1e-05) * gains[1:2, :]).astype(BF16)
        for step in range(1, HELPERS):
            send(
                f"n{step}{image}",
                normed.at[0, image],
                normed.at[HELPERS - step, image],
                helper_at(step),
            )

    arrived("w1", "w2", "w3")
    for step in (1, 3, 2):
        send(
            f"wx{step}",
            w_all.at[pl.ds(1, 3), weight_rows(my_x), weight_half(core)],
            w_all.at[pl.ds(1, 3), weight_rows(my_x), weight_half(core)],
            chip_at(0, step),
            seen=w_all.at[pl.ds(1, 3), weight_rows((my_x + X - step) % X), weight_half(core)],
        )

    arrived("x--", "x++")
    send("x2z+", mine.at[2, 2, :, over_z], mine.at[1, 2, :, over_z], north)
    send("x2z-", mine.at[2, 2, :, over_z], mine.at[3, 2, :, over_z], south)
    share(2, 2)
    first_x, last_x = my_x == 0, my_x == X - 1
    arrived("x+z+")
    send("c0z", mine.at[1, 3, :, over_z], mine.at[0, 3, :, over_z], north, first_x)
    arrived("x-z-")
    send("c3z", mine.at[3, 1, :, over_z], mine.at[4, 1, :, over_z], south, last_x)
    @pl.loop(0, SLOTS)
    def _(m):
        offset, layer = slot_owner(m // 2, m % 2, core)
        target = 2 * ((chip + offset + OWNERS // 2) % (OWNERS // 2)) + (layer + core) % 2
        target = 2 * jnp.where(m == SLOTS - 1, (me + OWNERS // 2) % OWNERS, target)
        code = jnp.int32(0)
        for image in range(IMAGES):
            for s in range(SLOTS):
                past = part[image, s] - target
                hit = jnp.logical_and(past >= 0, past <= 1)
                code = jnp.where(hit, 2 * image + past, code)
        own_bits[m] = code // 2
        partner_bits[m] = code % 2

    arrived("z+x+")
    send("z+x++", mine.at[1, 3, :, over_x], mine.at[1, 2, :, over_x], east)
    send("c0x", mine.at[1, 3, :, over_x], mine.at[0, 3, :, over_x], north, first_x)
    arrived("z-x-")
    send("z-x--", mine.at[3, 1, :, over_x], mine.at[3, 2, :, over_x], west)
    send("c3x", mine.at[3, 1, :, over_x], mine.at[4, 1, :, over_x], south, last_x)
    share(1, 3)
    share(3, 1)
    for image in range(IMAGES):
        arrived(*[f"n{step}{image}" for step in range(1, HELPERS)])
        rows = normed[:, image].reshape(PATCHES, D)
        q_tiles = pair_tiles(dot_nt(rows, cproj_v[0]) * HEAD ** (-0.5), None)
        for parity in range(2):
            for h in range(HEADS):
                for step in range(HELPERS):
                    qbuf[parity, image, h, rows_of(step)] = q_tiles[parity][h][
                        ROWS * step : ROWS * (step + 1)
                    ]

    def context_copy(n, step):
        return pltpu.make_async_remote_copy(
            src_ref=ctxbuf.at[n, rows_of(step)],
            dst_ref=ctx_recv.at[HELPERS - 1 - step, n],
            send_sem=c_send.at[n, step - 1],
            recv_sem=c_recv.at[n, step - 1],
            device_id=helper_at(step),
            device_id_type=MESH,
        )

    def slot_tiles(pair, parity):
        m = 2 * pair + parity
        offset, layer = slot_owner(pair, parity, core)
        col = (offset + 2 * X) % X
        row = (my_x + offset + 2 * X) // X
        image, which = own_bits[m], partner_bits[m]
        kv = jnp.where(
            which == 1, gathered[layer, row, col, 1], gathered[layer, row, col, 0]
        )
        return [
            (qbuf[parity, image, h], kv[:, 128 * h : 128 * (h + 1)]) for h in range(HEADS)
        ]

    def finish_pair(n, even, odd):
        for t, tile in enumerate(join_contexts(even, odd)):
            ctxbuf[n, :, 128 * t : 128 * (t + 1)] = tile
        for step in (2, 1, 3):
            context_copy(n, step).start()

    def work_pairs(first, last):
        @pl.loop(first, last)
        def _(n):
            pair = pair_at(n, my_x, core)
            contexts = head_contexts(slot_tiles(pair, 0) + slot_tiles(pair, 1))
            finish_pair(n, contexts[:HEADS], contexts[HEADS:])

    def y_copy(first, count):
        return pltpu.make_async_copy(
            y.at[pl.ds(2 * first, 2 * count)], y_out.at[pl.ds(2 * first, 2 * count)], y_sem.at[first]
        )

    def project(first, count):
        @pl.loop(first, first + count)
        def _(n):
            for step in range(1, HELPERS):
                context_copy(n, step).wait()

        for parity in range(2):
            start, weight_rows = (0, slice(PAD, None)) if parity == 0 else (128, slice(0, 256))
            cut = slice(start, start + 256)
            blocks = [ctxbuf[first : first + count, rows_of(0), cut]]
            blocks += [ctx_recv[rel - 1, first : first + count, :, cut] for rel in range(1, HELPERS)]
            lhs = jnp.concatenate([block.reshape(count * ROWS, 256) for block in blocks], axis=1)
            rhs = jnp.concatenate([w_all[rel, weight_rows] for rel in range(HELPERS)], axis=0)
            terms = dot(lhs, rhs)
            for i in range(count):
                n = first + i
                last = n == PAIRS - 1
                if last and parity == 1:
                    y[SLOTS] = jnp.zeros((ROWS, D), BF16)
                    continue
                m = SLOTS - 1 if last else 2 * pair_at(n, my_x, core) + parity
                y[2 * n + parity] = (
                    terms[ROWS * i : ROWS * (i + 1)] + mixed_v[own_bits[m]]
                ).astype(BF16)
        y_copy(first, count).start()

    arrived("s10", "s30", "s23", "s21")
    work_pairs(0, 4)
    arrived("z+x-", "x-z+")
    share(1, 1)
    arrived("z-x+", "x+z-")
    share(3, 3)
    arrived("s22", "s13", "s31", "s11", "s33", "s20")
    work_pairs(4, 8)
    arrived("far")
    far_tiles = [
        (qbuf[0, own_bits[SLOTS - 1], h], far_recv[:, 128 * h : 128 * (h + 1)]) for h in range(HEADS)
    ]
    finish_pair(PAIRS - 1, head_contexts(far_tiles), None)
    arrived("wx1", "wx2", "wx3")
    send(
        "ws",
        w_all.at[pl.ds(1, 3), pl.ds(PAD, COLS), weight_half(core)],
        w_all.at[pl.ds(1, 3), pl.ds(PAD, COLS), weight_half(core)],
        sibling,
        seen=w_all.at[pl.ds(1, 3), pl.ds(PAD, COLS), weight_half(1 - core)],
    )
    arrived("z+x++", "x2z+")
    share(1, 2)
    arrived("z-x--", "x2z-")
    share(3, 2)
    arrived("c0z", "c3z", "c0x", "c3x")
    share(0, 3, first_x)
    share(4, 1, last_x)
    arrived("ws")
    loads[4].wait()
    project(0, 4)
    arrived("s12", "s32", "s03", "s41")
    work_pairs(8, 10)
    project(4, 4)
    project(8, 3)

    for sent, _, when in copies.values():
        if when is None:
            sent().wait_send()
        else:
            pl.when(when)(lambda: sent().wait_send())

    y_copy(0, 4).wait()
    y_copy(4, 4).wait()
    y_copy(8, 3).wait()


def place_kernel(part, y, out, steps, out_sem):
    me = lax.axis_index("owner")

    @pl.loop(0, PAIRS - 1)
    def _(n):
        steps[pair_at(n, (me // 2) % X, me % 2)] = n

    def result_copy(index, image, slot):
        return pltpu.make_async_copy(y.at[index], out.at[image, slot], out_sem.at[image, slot])

    for image in range(IMAGES):

        @pl.loop(0, SLOTS, unroll=7)
        def _(slot):
            p = part[image, slot]
            owner = lax.div(jnp.maximum(p, 0), 2)
            parity = owner % 2
            chips = OWNERS // 2
            offset = (owner // 2 - me // 2 + chips + chips // 2) % chips - chips // 2
            size = jnp.abs(offset)
            group = jnp.where(size == 4, 0, jnp.where(size == 1, 1, jnp.where(size == 3, 2, 3)))
            pair = 2 * group + jnp.where(offset < 0, 1, 0)
            pair = jnp.where(size == 5, jnp.where(offset == 10 * (me % 2) - 5, 8, 9), pair)
            pair = jnp.where(size == 0, 9, pair)
            index = 2 * steps[jnp.minimum(pair, 9)] + parity
            index = jnp.where(size == chips // 2, SLOTS - 1, index)

            index = jnp.where(p >= 0, index, SLOTS)
            result_copy(index, image, slot).start()

    for image in range(IMAGES):

        @pl.loop(0, SLOTS, unroll=7)
        def _(slot):
            result_copy(0, image, slot).wait()


def local(states, partners, self_proj, self_out, cross_proj, cross_out, gains):
    any_spec = pl.BlockSpec(memory_space=pl.ANY)
    smem = pl.BlockSpec(memory_space=pltpu.SMEM)
    vmem = pl.BlockSpec(memory_space=pltpu.VMEM)
    dma = pltpu.SemaphoreType.DMA
    y = pl.pallas_call(
        exchange_kernel,
        out_shape=jax.ShapeDtypeStruct((2 * PAIRS, ROWS, D), BF16),
        in_specs=[smem, any_spec, any_spec, any_spec, any_spec, any_spec, vmem],
        out_specs=any_spec,
        scratch_shapes=[
            pltpu.VMEM((IMAGES, PATCHES, D), BF16),
            pltpu.VMEM((3, COLS, D), BF16),
            pltpu.VMEM((3, COLS, D), BF16),
            pltpu.VMEM((COLS + 2 * PAD, D), BF16),
            pltpu.VMEM((IMAGES * PATCHES, D), BF16),
            pltpu.VMEM((IMAGES * PATCHES, D), BF16),
            pltpu.VMEM((2, IMAGES, PATCHES, LANES), BF16),
            pltpu.VMEM((PATCHES, LANES), BF16),
            pltpu.VMEM((PATCHES, LANES), BF16),
            pltpu.VMEM((2, 5, X, IMAGES, PATCHES, LANES), BF16),
            pltpu.VMEM((IMAGES, PATCHES, D), BF16),
            pltpu.VMEM((HELPERS - 1, IMAGES, ROWS, D), BF16),
            pltpu.VMEM((IMAGES, ROWS, D), F32),
            pltpu.VMEM((HELPERS, IMAGES, ROWS, D), BF16),
            pltpu.VMEM((2, IMAGES, HEADS, PATCHES, 2 * HEAD), BF16),
            pltpu.VMEM((PAIRS, PATCHES, LANES), BF16),
            pltpu.VMEM((HELPERS - 1, PAIRS, ROWS, LANES), BF16),
            pltpu.VMEM((HELPERS, COLS + 2 * PAD, D), BF16),
            pltpu.VMEM((2 * PAIRS, ROWS, D), BF16),
            pltpu.SMEM((SLOTS,), jnp.int32),
            pltpu.SMEM((SLOTS,), jnp.int32),
            dma((5,)),
            dma((PAIRS,)),
            pltpu.SemaphoreType.REGULAR((3,)),
            dma((COPIES,)),
            dma((COPIES,)),
            dma((PAIRS, 3)),
            dma((PAIRS, 3)),
        ],
        compiler_params=pltpu.CompilerParams(
            collective_id=0, has_side_effects=True, vmem_limit_bytes=VMEM_LIMIT
        ),
        name="exchange",
    )(
        partners,
        states,
        jnp.swapaxes(self_proj, 1, 2),
        self_out,
        jnp.swapaxes(cross_proj, 1, 2),
        cross_out,
        gains,
    )
    return pl.pallas_call(
        place_kernel,
        out_shape=jax.ShapeDtypeStruct((IMAGES, SLOTS, ROWS, D), BF16),
        in_specs=[smem, vmem],
        out_specs=any_spec,
        scratch_shapes=[
            pltpu.SMEM((PAIRS,), jnp.int32),
            dma((IMAGES, SLOTS)),
        ],
        compiler_params=pltpu.CompilerParams(vmem_limit_bytes=VMEM_LIMIT),
        name="place",
    )(partners, y)


def solution(mesh):
    return jax.shard_map(
        local,
        mesh=mesh,
        in_specs=(
            P("owner", None, None),
            P("owner", None),
            P(None, None, "helper"),
            P("helper", None),
            P(None, None, "helper"),
            P("helper", None),
            P(),
        ),
        out_specs=P("owner", None, "helper", None),
        check_vma=False,
    )
```
